32 devices in a mesh: occ: 8 (over z, x), aux: 4 (over y, core).
Axes of the slice: x: 2, y: 2, z: 4, core: 2. Of those that a mesh axis runs over, the one named last changes fastest.
Arguments:
- factors: bfloat16 [16, 256, 1024], P('occ', None, 'aux'), may hold values from -0.8984375 to 0.8984375
- occ_energy: float32 [16], replicated, may hold values from -3 to -0.5
- vir_energy: float32 [256], replicated, may hold values from 0.5 to 3
- i_slot: int32 [256], P('occ'), may hold values from 0 to 1
- j_slot: int32 [256], P('occ'), may hold values from 0 to 1
- partner_device: int32 [256, 1], P('occ'), may hold values from 0 to 7; in each aligned block of 32 rows (0 to 31, 32 to 63, ...) at most 6 rows name the same one
- pair_count: int32 [8], P('occ'), may hold values from 1 to 32, 230 in all
Outputs:
- gamma: float32 [16, 256, 1024], P('occ', None, 'aux')
- aux_matrix: float32 [1024, 1024], P('aux', 'occ')
The draws below stay inside these ranges and needn't reach their ends.
Inputs may be any that keep to these rules, and one draw needn't show every extreme that they name: `partner_device`: among the 32 pair slots of one occ index, at most 6 name the same partner device, and some index reaches 6.
All inputs are finite; a program needn't handle non-finite values. No bound on the sum of `pair_count` on one device may be relied on, other than what follows from the above.
Results may differ from the reference program's by a relative error of at most 0.0013.
Values may be sent and summed in bfloat16 or wider, within the bound.
A program may use at most 128 MiB of HBM per device.

```python
import math
import jax
import jax.numpy as jnp
import numpy as np
from jax import lax

V = 256
Q = 1024
OCC_DEV = 2
PAIR_DEV = 32
O = 16
PAIRS = 256
CAP = 6
N_OCC = 8


def set_ends(result, rng, least, top_value):
    longest = result.shape.index(max(result.shape))
    spots = []
    for shift in (0, 1):
        where = [jax.random.randint(jax.random.fold_in(rng, axis), (), 0, length) for axis, length in enumerate(result.shape)]
        where[longest] = (where[longest] + shift) % result.shape[longest]
        spots.append(tuple(where))
    return result.at[spots[0]].set(least).at[spots[1]].set(top_value)


def level_of(stream_key, shape, shards, least, high):
    level = 1.0
    for axis_at, blocks in shards:
        draws = jax.random.uniform(jax.random.fold_in(jax.random.fold_in(stream_key, 6), axis_at), (blocks,), jnp.float32, least / len(shards), high / len(shards))
        level = level * jnp.repeat(jnp.exp(draws), shape[axis_at] // blocks).reshape((-1,) + (1,) * (len(shape) - 1 - axis_at))
    return level


def split_up(number_of, total, reach, slope):
    weights = [(1 << 20) // math.isqrt(standing ** slope) + 1 for standing in range(2, number_of + 1)]
    spare, holding = total - reach - (number_of - 1), [1] * (number_of - 1)
    while spare > 0:
        free = [i for i in range(number_of - 1) if holding[i] < reach]
        pool, budget = sum([weights[i] for i in free]), spare
        for i in free:
            more = min(reach - holding[i], max(1, budget * weights[i] // pool), spare)
            holding[i] = holding[i] + more
            spare = spare - more
    return np.array([reach] + holding)


def ragged_sizes(stream_key, amount, total, limit, slope):
    if amount == 2:
        one = jax.random.randint(stream_key, (), max(1, total - limit), min(limit, total - 1) + 1)
        return jnp.stack([one, total - one])
    lengths = jnp.asarray(split_up(amount, total, limit, slope), jnp.int32)
    couples = (amount - 1) // 2
    giver, receiver = lengths[1:1 + 2 * couples:2], lengths[2:2 + 2 * couples:2]
    margin = jnp.minimum(giver - 1, limit - receiver)
    moved = jax.random.randint(jax.random.fold_in(stream_key, 1), (couples,), 0, 1 << 20) % (margin + 1)
    lengths = lengths.at[1:1 + 2 * couples:2].set(giver - moved).at[2:2 + 2 * couples:2].set(receiver + moved)
    return lengths[jax.random.permutation(jax.random.fold_in(stream_key, 2), amount)]


def shared_out(own_key, own, number, rows, count, top, limit, lean):
    sequence = jax.random.permutation(own_key, count)
    packed, usual = shares(count, rows * top, limit, lean, True), shares(count, rows * top, limit, lean, False)
    places = jnp.arange(count)

    def named(lengths, turn):
        used = int((lengths > 0).sum())
        fixed = max(1, used // 4)
        passed = fixed + (places - fixed + turn * (used - fixed)) % max(1, count - fixed)
        return jnp.zeros((count,), jnp.int32).at[sequence[jnp.where(places < fixed, places, passed)]].set(jnp.asarray(lengths, jnp.int32))

    lengths = jnp.where(number % 4 == 0, named(packed, number // 4), named(usual, number - number // 4 - 1))
    mixed = jax.random.permutation(jax.random.fold_in(own, 3), count)
    source_of, receiver = mixed[0:count // 2 * 2:2], mixed[1:count // 2 * 2:2]
    room = jnp.minimum(lengths[source_of] - 1, limit - lengths[receiver]) // 2
    room = jnp.where((source_of == sequence[0]) | (receiver == sequence[0]) | (lengths[receiver] == 0), 0, jnp.maximum(room, 0))
    passed = jax.random.randint(jax.random.fold_in(own, 4), (count // 2,), 0, 1 << 20) % (room + 1)
    lengths = lengths.at[source_of].add(-passed).at[receiver].add(passed)
    items = jnp.searchsorted(jnp.cumsum(lengths), jnp.arange(rows * top), side="right").astype(jnp.int32)
    table = items.reshape(top, rows).T
    table = table[jax.random.permutation(jax.random.fold_in(own, 1), rows)]
    turn = jax.random.randint(jax.random.fold_in(own, 2), (rows, 1), 0, top)
    return jnp.take_along_axis(table, (jnp.arange(top)[None, :] + turn) % top, axis=1)


def shares(count, total, most, slope, full):
    loads = [(1 << 20) // math.isqrt(grade ** slope) + 1 for grade in range(1, count + 1)]
    largest = most if full else min(most, max(-(-total // count), total * loads[0] // sum(loads)))
    least = 1 if total - largest >= count - 1 else 0
    given, rest = [largest] + [least] * (count - 1), total - largest - least * (count - 1)
    while rest > 0:
        candidates = [i for i in range(1, count) if given[i] < largest] or [i for i in range(1, count) if given[i] < most]
        whole, remaining = sum([loads[i] for i in candidates]), rest
        for i in candidates:
            more = min(most - given[i], max(1, remaining * loads[i] // whole), rest)
            given[i] = given[i] + more
            rest = rest - more
    return np.array(given)


def gaussian(own_key, extent, scale, most, pieces=(), kind=jnp.bfloat16):
    values = scale * jax.random.normal(own_key, extent, jnp.float32)
    if pieces:
        values = values * level_of(own_key, extent, pieces, -0.22, 0.18)
    return jnp.clip(values, -most, most).astype(kind)


def setup_inputs(seed: int = 0) -> dict:
    arg_keys = jax.random.split(jax.random.key(seed), 8)
    factors = gaussian(arg_keys[0], (O, V, Q), 0.15, 0.8984375, ((0, 8), (2, 4)))
    occ_energy = jnp.clip(jax.random.uniform(arg_keys[1], (O,), jnp.float32, -3.0, -0.5), -3.0, -0.5)
    vir_energy = jnp.clip(jax.random.uniform(arg_keys[2], (V,), jnp.float32, 0.5, 3.0), 0.5, 3.0)
    i_slot = set_ends(jax.random.randint(arg_keys[3], (PAIRS,), 0, OCC_DEV), jax.random.fold_in(arg_keys[3], 1), 0, OCC_DEV - 1).astype(jnp.int32)
    j_slot = set_ends(jax.random.randint(arg_keys[4], (PAIRS,), 0, OCC_DEV), jax.random.fold_in(arg_keys[4], 1), 0, OCC_DEV - 1).astype(jnp.int32)
    partner_device_keys = jax.random.split(jax.random.fold_in(arg_keys[5], 1), PAIRS // PAIR_DEV)
    partner_device_turns = jax.random.permutation(jax.random.fold_in(arg_keys[5], 3), PAIRS // PAIR_DEV)
    partner_device = jax.vmap(lambda own, number: shared_out(jax.random.fold_in(arg_keys[5], 2), own, number, PAIR_DEV, N_OCC, 1, CAP, 2))(partner_device_keys, partner_device_turns).reshape((PAIRS, 1))
    pair_count = ragged_sizes(arg_keys[6], N_OCC, N_OCC * PAIR_DEV * 9 // 10, PAIR_DEV, 2).astype(jnp.int32)
    return dict(factors=factors, occ_energy=occ_energy, vir_energy=vir_energy, i_slot=i_slot, j_slot=j_slot, partner_device=partner_device, pair_count=pair_count)


def reference(factors, occ_energy, vir_energy, i_slot, j_slot, partner_device, pair_count):
    orbitals = OCC_DEV * N_OCC
    total_pairs = N_OCC * PAIR_DEV
    pair_ids = jnp.arange(total_pairs, dtype=jnp.int32)
    owners = (pair_ids // PAIR_DEV).astype(jnp.int32)
    living = (pair_ids % PAIR_DEV) < pair_count[owners]
    row_own = (owners * OCC_DEV + i_slot).astype(jnp.int32)
    row_far = (partner_device[:, 0] * OCC_DEV + j_slot).astype(jnp.int32)

    def visit(gamma, item):
        own_row, far_row, is_alive = item
        own_block = factors[own_row]
        far_block = factors[far_row]
        intersection = jnp.dot(own_block, far_block.T, preferred_element_type=jnp.float32)
        denominator = vir_energy[:, None] + vir_energy[None, :] - occ_energy[own_row] - occ_energy[far_row]
        amplitude = jnp.where(is_alive, intersection / denominator, jnp.zeros_like(intersection)).astype(jnp.bfloat16)
        gamma = gamma.at[own_row].add(jnp.dot(amplitude, far_block, preferred_element_type=jnp.float32))
        back_term = jnp.dot(amplitude.T, own_block, preferred_element_type=jnp.float32).astype(jnp.bfloat16)
        back_term = lax.optimization_barrier(back_term).astype(jnp.float32)
        gamma = gamma.at[far_row].add(back_term)
        return gamma, None

    start_gamma = jnp.zeros((orbitals, V, Q), jnp.float32)
    gamma = lax.scan(visit, start_gamma, (row_own, row_far, living))[0]
    rounded = gamma.astype(jnp.bfloat16).reshape(orbitals * V, Q)
    cross = jnp.dot(rounded.T, factors.reshape(orbitals * V, Q), preferred_element_type=jnp.float32)
    factor_scale = float(orbitals * V) ** -0.5
    return gamma, (cross + cross.T) * factor_scale
```

```python
import jax
import jax.numpy as jnp
from jax import lax
from jax.experimental import pallas as pl
from jax.experimental.pallas import tpu as pltpu
from jax.sharding import PartitionSpec as P

MESH = pl.DeviceIdType.MESH
f32 = jnp.float32
bf16 = jnp.bfloat16


def slot_body(factors, occ_energy, vir_energy, i_slot, j_slot, partner_device, pair_count):
    held, virtuals, columns = factors.shape
    pair_slots = i_slot.shape[0]
    occ_count = lax.axis_size("occ")
    capacity = max(2, (3 * pair_slots // 2 + occ_count - 1) // occ_count)
    slot_total = occ_count * capacity
    device_index = lax.axis_index("occ")
    pair_order = jnp.arange(pair_slots, dtype=jnp.int32)
    living = pair_order < pair_count[0]
    target = partner_device[:, 0]
    earlier = (
        (target[:, None] == target[None, :])
        & living[None, :]
        & (pair_order[None, :] < pair_order[:, None])
    )
    slot_rank = jnp.sum(earlier.astype(jnp.int32), axis=1)
    slot_index = target * capacity + slot_rank
    slot_hit = (slot_index[:, None] == jnp.arange(slot_total, dtype=jnp.int32)[None, :]) & living[
        :, None
    ]
    requests = jnp.sum(jnp.where(slot_hit, j_slot[:, None] + 1, 0), axis=0) - 1
    wanted = lax.all_to_all(requests, "occ", split_axis=0, concat_axis=0, tiled=True)
    wanted_hit = (wanted[:, None] == jnp.arange(held, dtype=jnp.int32)[None, :]).astype(
        jnp.bfloat16
    )
    far_index = target * held + j_slot
    piece = lax.all_gather(factors, "occ", axis=0, tiled=True)
    count = piece.shape[0]
    hit = (far_index[:, None] == jnp.arange(count, dtype=jnp.int32)[None, :]).astype(jnp.bfloat16)
    gathered = jnp.dot(
        hit, piece.reshape(count, virtuals * columns), preferred_element_type=jnp.float32
    )
    partner_blocks = gathered.astype(jnp.bfloat16).reshape(pair_slots, virtuals, columns)
    own_blocks = factors[i_slot]
    orbitals = occ_energy.shape[0]
    table = jnp.arange(orbitals, dtype=jnp.int32)
    own_index = device_index * held + i_slot
    energy_own = jnp.sum(
        jnp.where(own_index[:, None] == table[None, :], occ_energy[None, :], 0.0), axis=1
    )
    energy_far = jnp.sum(
        jnp.where(far_index[:, None] == table[None, :], occ_energy[None, :], 0.0), axis=1
    )
    denominator = (
        vir_energy[None, :, None]
        + vir_energy[None, None, :]
        - energy_own[:, None, None]
        - energy_far[:, None, None]
    )
    partial_value = jnp.einsum(
        "pvq,pwq->pvw", own_blocks, partner_blocks, preferred_element_type=jnp.float32
    )
    summed = lax.psum(partial_value, "aux")
    amplitude = jnp.where(living[:, None, None], summed / denominator, 0.0).astype(jnp.bfloat16)
    local_terms = jnp.einsum(
        "pvw,pwq->pvq", amplitude, partner_blocks, preferred_element_type=jnp.float32
    )
    owner_hit = (i_slot[:, None] == jnp.arange(held, dtype=jnp.int32)[None, :]).astype(jnp.float32)
    gamma_local = jnp.einsum("po,pvq->ovq", owner_hit, local_terms, precision=lax.Precision.HIGHEST)
    return_terms = jnp.einsum(
        "pwv,pwq->pvq", amplitude, own_blocks, preferred_element_type=jnp.float32
    ).astype(jnp.bfloat16)
    placed = jnp.dot(
        slot_hit.astype(jnp.bfloat16).T,
        return_terms.reshape(pair_slots, virtuals * columns),
        preferred_element_type=jnp.float32,
    )
    placed = placed.astype(jnp.bfloat16).reshape(slot_total, virtuals, columns)
    returned = lax.all_to_all(placed, "occ", split_axis=0, concat_axis=0, tiled=True)
    gathered_back = jnp.dot(
        wanted_hit.T,
        returned.reshape(slot_total, virtuals * columns),
        preferred_element_type=jnp.float32,
    )
    gamma = gamma_local + gathered_back.reshape(held, virtuals, columns)
    rounded = gamma.astype(jnp.bfloat16)
    stacked = jnp.stack([rounded, factors])
    gamma_rows = rounded.reshape(held * virtuals, columns)
    factor_flat = factors.reshape(held * virtuals, columns)
    piece = lax.all_gather(stacked, "aux", axis=3, tiled=True)
    width_here = piece.shape[3]
    gamma_piece = piece[0].reshape(held * virtuals, width_here)
    factor_piece = piece[1].reshape(held * virtuals, width_here)
    first = jnp.dot(gamma_rows.T, factor_piece, preferred_element_type=jnp.float32)
    second = jnp.dot(factor_flat.T, gamma_piece, preferred_element_type=jnp.float32)
    terms = first + second
    shared = lax.psum_scatter(terms, "occ", scatter_dimension=1, tiled=True)
    factor_scale = float(orbitals * virtuals) ** (-0.5)
    return (gamma, shared * factor_scale)


def nt(a, b):
    return lax.dot_general(a, b, (((1,), (1,)), ((), ())), preferred_element_type=f32)


def tn(a, b):
    return lax.dot_general(a, b, (((0,), (0,)), ((), ())), preferred_element_type=f32)


def kernel(
    f_ref, cnt_ref, e_ref, vcol_ref, vrow_ref,
    gamma_ref, aux_ref,
    kbuf, lbuf, kh, cnt, gacc, gsend, grecv, gfull, gsib, asend, arecv, tsend, trecv,
    ky_s, ky_r, ksib_s, ksib_r, z_s, z_r, x_s, x_r, s_s, s_r,
    cnt_s, cnt_r, g_s, g_r, gs_s, gs_r, a_s, a_r, t_s, t_r,
):
    occ_count = lax.axis_size("occ")
    lines = occ_count // 2
    held, virtuals, width = f_ref.shape
    half = virtuals // 2
    o = lax.axis_index("occ")
    a = lax.axis_index("aux")
    z, x = o // 2, o % 2
    y, c = a // 2, a % 2
    oy, oc, ox = 1 - y, 1 - c, 1 - x

    def dev(occ, aux):
        return {"occ": occ, "aux": aux}

    y_peer, sibling = dev(o, oy * 2 + c), dev(o, y * 2 + oc)
    x_peer = dev(z * 2 + ox, a)

    def rcopy(src, dst, ss, rs, target):
        return pltpu.make_async_remote_copy(
            src_ref=src, dst_ref=dst, send_sem=ss, recv_sem=rs, device_id=target, device_id_type=MESH
        )

    barrier = pltpu.get_barrier_semaphore()
    for s in range(1, occ_count):
        pl.semaphore_signal(barrier, inc=1, device_id=dev((o + s) % occ_count, a), device_id_type=MESH)
    pl.semaphore_signal(barrier, inc=1, device_id=y_peer, device_id_type=MESH)
    pl.semaphore_signal(barrier, inc=1, device_id=sibling, device_id_type=MESH)
    ta = o // 2
    for h in range(2):
        @pl.when(jnp.logical_or(ta != a, o != 2 * a + h))
        def _():
            pl.semaphore_signal(barrier, inc=1, device_id=dev(2 * a + h, ta), device_id_type=MESH)
    pl.semaphore_wait(barrier, occ_count + 1 + jnp.where(ta != a, 2, 1))

    def ky(r):
        return rcopy(f_ref.at[r], kbuf.at[c, y, r], ky_s.at[r], ky_r.at[r], y_peer)

    def ky_wait(r):
        rcopy(f_ref.at[r], kbuf.at[c, oy, r], ky_s.at[r], ky_r.at[r], y_peer).wait_recv()

    def ksib(n, yy, r):
        return rcopy(kbuf.at[c, yy, r], kbuf.at[c, yy, r], ksib_s.at[n], ksib_r.at[n], sibling)

    def ksib_wait(n, yy, r):
        rcopy(kbuf.at[oc, yy, r], kbuf.at[oc, yy, r], ksib_s.at[n], ksib_r.at[n], sibling).wait_recv()

    def item(oo, yy):
        return lbuf.at[oo, c, yy]

    def z_copy(d, zz, yy):
        oo = zz * 2 + x
        return rcopy(item(oo, yy), item(oo, yy), z_s.at[d, zz, yy], z_r.at[zz, yy], dev((z + 1 - 2 * d) * 2 + x, a))

    def x_copy(zz, yy):
        oo = zz * 2 + x
        return rcopy(item(oo, yy), item(oo, yy), x_s.at[zz, yy], x_r.at[zz, yy], x_peer)

    def x_wait(zz, yy):
        oo = zz * 2 + ox
        rcopy(item(oo, yy), item(oo, yy), x_s.at[zz, yy], x_r.at[zz, yy], x_peer).wait_recv()

    def s_copy(oo, yy):
        return rcopy(item(oo, yy), item(oo, yy), s_s.at[oo, yy], s_r.at[oo, yy], sibling)

    def s_wait(oo, yy):
        there = lbuf.at[oo, oc, yy]
        rcopy(there, there, s_s.at[oo, yy], s_r.at[oo, yy], sibling).wait_recv()

    def forward(zz, yy, right, left):
        @pl.when(jnp.logical_and(right, z + 1 < lines))
        def _():
            z_copy(0, zz, yy).start()

        @pl.when(jnp.logical_and(left, z > 0))
        def _():
            z_copy(1, zz, yy).start()

        x_copy(zz, yy).start()
        s_copy(zz * 2 + x, yy).start()

    ky(oy).start()
    lbuf[o, c, y] = f_ref[y]
    forward(z, y, True, True)
    ky(y).start()
    kbuf[c, y] = f_ref[...]
    ksib(0, y, 0).start()
    ksib(1, y, 1).start()
    cnt[o] = cnt_ref[...]

    def cnt_copy(oo):
        return rcopy(cnt_ref, cnt.at[o], cnt_s.at[oo], cnt_r.at[o], dev(oo, a))

    for s in range(1, occ_count):
        cnt_copy((o + s) % occ_count).start()

    ky_wait(y)
    lbuf[o, c, oy] = kbuf[c, oy, y]
    forward(z, oy, True, True)
    ksib(2, oy, y).start()
    ky_wait(oy)
    ksib(3, oy, oy).start()

    gacc[...] = jnp.zeros_like(gacc)
    for s in range(1, occ_count):
        oo = (o + s) % occ_count
        rcopy(cnt_ref, cnt.at[oo], cnt_s.at[oo], cnt_r.at[oo], dev(oo, a)).wait_recv()
    ksib_wait(0, y, 0)
    ksib_wait(1, y, 1)
    ksib_wait(2, oy, y)
    ksib_wait(3, oy, oy)
    for cc in range(2):
        for yy in range(2):
            for k in range(2):
                kh[cc, yy, k * half:(k + 1) * half] = kbuf[cc, yy, k, pl.ds(c * half, half)]
    vhalf = vcol_ref[pl.ds(c * half, half)]
    side = jnp.concatenate([vhalf - e_ref[2 * o], vhalf - e_ref[2 * o + 1]], axis=0)
    vrow = vrow_ref[...]
    rows8 = lax.broadcasted_iota(jnp.int32, cnt_ref.shape, 0)
    lanes8 = lax.broadcasted_iota(jnp.int32, cnt_ref.shape, 1)

    def pick(tile, row, lane):
        here = jnp.logical_and(rows8 == row, lanes8 == lane)
        return jnp.sum(jnp.where(here, tile, 0.0), keepdims=True)

    def work(oo):
        far = 2 * oo + y
        inter = nt(kh[0, 0], lbuf[oo, 0, 0])
        inter += nt(kh[0, 1], lbuf[oo, 0, 1])
        inter += nt(kh[1, 0], lbuf[oo, 1, 0])
        inter += nt(kh[1, 1], lbuf[oo, 1, 1])
        amplitude = (inter / (side + (vrow - e_ref[far]))).astype(bf16)
        mine, theirs = cnt[o], cnt[oo]
        w1 = [pick(mine, k, far) for k in range(2)]
        w2 = [pick(theirs, y, 2 * o + k) for k in range(2)]
        for cc in range(2):
            for yy in range(2):
                term = jnp.dot(amplitude, lbuf[oo, cc, yy], preferred_element_type=f32)
                for k in range(2):
                    part = term[k * half:(k + 1) * half]
                    gacc[cc, yy, k * half:(k + 1) * half] += (
                        w1[k] * part + w2[k] * part.astype(bf16).astype(f32)
                    )

    def place(d, sign):
        zz = z - d + 2 * d * sign
        ok = jnp.logical_and(jnp.logical_and(zz >= 0, zz < lines), jnp.logical_or(d > 0, sign == 0))
        return zz, ok

    def step(d, carry):
        @pl.when(d < lines)
        def _():
            for n in range(2):
                yy = (y + n) % 2
                for sign in range(2):
                    zz, ok = place(d, sign)

                    @pl.when(ok)
                    def _():
                        z_copy(0, zz, yy).wait_recv()
                        forward(zz, yy, sign == 0, sign == 1)

        before = d - 1
        for sign in range(2):
            zz, ok = place(before, sign)

            @pl.when(ok)
            def _():
                for n in range(2):
                    yy = (y + n) % 2
                    x_wait(zz, yy)
                    s_copy(zz * 2 + ox, yy).start()

        def each(n, carry):
            zz, ok = place(before, n // 2)
            oo = zz * 2 + (x + n) % 2

            @pl.when(ok)
            def _():
                s_wait(oo, 0)
                s_wait(oo, 1)
                work(oo)

            return carry

        lax.fori_loop(0, 4, each, 0)
        return carry

    lax.fori_loop(1, lines + 1, step, 0)

    def g_copy(cc):
        return rcopy(gsend.at[cc], grecv.at[cc], g_s.at[cc], g_r.at[cc], y_peer)

    for n in range(2):
        cc = (c + 1 + n) % 2
        gsend[cc] = gacc[cc, oy].astype(bf16)
        g_copy(cc).start()
    for n in range(2):
        cc = (c + 1 + n) % 2
        g_copy(cc).wait_recv()
        gfull[n] = gacc[cc, y] + grecv[cc].astype(f32)
        if n == 0:
            gs_copy = rcopy(gfull.at[0], gsib, gs_s, gs_r, sibling)
            gs_copy.start()
    for k in range(2):
        gamma_ref[k, pl.ds(c * half, half)] = gfull[1, k * half:(k + 1) * half]
    gs_copy.wait_recv()
    for k in range(2):
        gamma_ref[k, pl.ds(oc * half, half)] = gsib[k * half:(k + 1) * half]
    rounded = gamma_ref[...].reshape(held * virtuals, width).astype(bf16)

    out_width = aux_ref.shape[1]

    def a_copy(oo):
        return rcopy(asend.at[oo], arecv.at[o], a_s.at[oo], a_r.at[o], dev(oo, a))

    for n in range(4):
        block = (ta + n) % 4
        terms = tn(rounded, kbuf[block % 2, block // 2].reshape(held * virtuals, width))
        for h in range(2):
            oo = 2 * block + h
            part = terms[:, h * out_width:(h + 1) * out_width]
            asend[oo] = part.astype(bf16)

            @pl.when(oo == o)
            def _():
                aux_ref[...] = part

            @pl.when(oo != o)
            def _():
                a_copy(oo).start()

    total = aux_ref[...]
    for s in range(1, occ_count):
        oo = (o + s) % occ_count
        rcopy(asend.at[oo], arecv.at[oo], a_s.at[oo], a_r.at[oo], dev(oo, a)).wait_recv()
        total += arecv[oo].astype(f32)
    for h in range(2):
        tsend[h] = total[h * out_width:(h + 1) * out_width]

    def t_copy(h):
        return rcopy(tsend.at[h], trecv.at[o % 2], t_s.at[h], t_r.at[o % 2], dev(2 * a + h, ta))

    for h in range(2):
        far = jnp.logical_or(ta != a, o != 2 * a + h)

        @pl.when(far)
        def _():
            t_copy(h).start()

        @pl.when(jnp.logical_not(far))
        def _():
            trecv[o % 2] = tsend[h]

    scale = float(occ_count * held * virtuals) ** (-0.5)
    for h in range(2):
        @pl.when(jnp.logical_or(ta != a, o != 2 * a + h))
        def _():
            rcopy(tsend.at[h], trecv.at[h], t_s.at[h], t_r.at[h], dev(2 * a + h, ta)).wait_recv()

        rows = slice(h * out_width, (h + 1) * out_width)
        aux_ref[rows] = (total[rows] + trecv[h].T) * scale

    for r in range(2):
        ky(r).wait_send()
        g_copy(r).wait_send()
    ksib(0, y, 0).wait_send()
    ksib(1, y, 1).wait_send()
    ksib(2, oy, y).wait_send()
    ksib(3, oy, oy).wait_send()
    gs_copy.wait_send()
    for s in range(1, occ_count):
        oo = (o + s) % occ_count
        cnt_copy(oo).wait_send()
        a_copy(oo).wait_send()
    for h in range(2):
        @pl.when(jnp.logical_or(ta != a, o != 2 * a + h))
        def _():
            t_copy(h).wait_send()

    def drain(zz, carry):
        for yy in range(2):
            @pl.when(jnp.logical_and(zz <= z, z + 1 < lines))
            def _():
                z_copy(0, zz, yy).wait_send()

            @pl.when(jnp.logical_and(zz >= z, z > 0))
            def _():
                z_copy(1, zz, yy).wait_send()

            x_copy(zz, yy).wait_send()
            s_copy(zz * 2, yy).wait_send()
            s_copy(zz * 2 + 1, yy).wait_send()
        return carry

    lax.fori_loop(0, lines, drain, 0)


def table_body(factors, occ_energy, vir_energy, i_slot, j_slot, partner_device, pair_count):
    held, virtuals, width = factors.shape
    slots = i_slot.shape[0]
    occ_count = lax.axis_size("occ")
    lines = occ_count // 2
    out_width = 4 * width // occ_count
    living = jnp.arange(slots, dtype=jnp.int32) < pair_count[0]
    far = partner_device[:, 0] * held + j_slot
    row_hit = jnp.logical_and(
        i_slot[None, :, None] == jnp.arange(8, dtype=jnp.int32)[:, None, None], living[None, :, None]
    )
    col_hit = far[None, :, None] == jnp.arange(128, dtype=jnp.int32)[None, None, :]
    counts = jnp.sum(jnp.logical_and(row_hit, col_hit).astype(f32), axis=1)
    vmem = pl.BlockSpec(memory_space=pltpu.VMEM)
    dma = pltpu.SemaphoreType.DMA
    return pl.pallas_call(
        kernel,
        out_shape=(
            jax.ShapeDtypeStruct((held, virtuals, width), f32),
            jax.ShapeDtypeStruct((width, out_width), f32),
        ),
        in_specs=[vmem, vmem, pl.BlockSpec(memory_space=pltpu.SMEM), vmem, vmem],
        out_specs=(vmem, vmem),
        scratch_shapes=[
            pltpu.VMEM((2, 2, held, virtuals, width), bf16),
            pltpu.VMEM((occ_count, 2, 2, virtuals, width), bf16),
            pltpu.VMEM((2, 2, virtuals, width), bf16),
            pltpu.VMEM((occ_count, 8, 128), f32),
            pltpu.VMEM((2, 2, virtuals, width), f32),
            pltpu.VMEM((2, virtuals, width), bf16),
            pltpu.VMEM((2, virtuals, width), bf16),
            pltpu.VMEM((2, virtuals, width), f32),
            pltpu.VMEM((virtuals, width), f32),
            pltpu.VMEM((occ_count, width, out_width), bf16),
            pltpu.VMEM((occ_count, width, out_width), bf16),
            pltpu.VMEM((2, out_width, out_width), f32),
            pltpu.VMEM((2, out_width, out_width), f32),
            dma((2,)), dma((2,)), dma((4,)), dma((4,)),
            dma((2, lines, 2)), dma((lines, 2)), dma((lines, 2)), dma((lines, 2)),
            dma((occ_count, 2)), dma((occ_count, 2)),
            dma((occ_count,)), dma((occ_count,)), dma((2,)), dma((2,)), dma, dma,
            dma((occ_count,)), dma((occ_count,)), dma((2,)), dma((2,)),
        ],
        compiler_params=pltpu.CompilerParams(
            collective_id=0, has_side_effects=True, vmem_limit_bytes=40 * 1024 * 1024
        ),
    )(factors, counts, occ_energy, vir_energy[:, None], vir_energy[None, :])


def body(*operands):
    factors, i_slot = operands[0], operands[3]
    held, virtuals, width = factors.shape
    occ_count, aux_count = lax.axis_size("occ"), lax.axis_size("aux")
    orbitals = held * occ_count
    fits = (
        held == 2 and aux_count == 4 and occ_count == 2 * aux_count and orbitals <= 128
        and orbitals * orbitals <= occ_count * i_slot.shape[0]
        and virtuals == width and width % 256 == 0
    )
    return table_body(*operands) if fits else slot_body(*operands)


def solution(mesh):
    placed = (P("occ", None, "aux"), P(), P(), P("occ"), P("occ"), P("occ", None), P("occ"))
    return jax.shard_map(
        body,
        mesh=mesh,
        in_specs=placed,
        out_specs=(P("occ", None, "aux"), P("aux", "occ")),
        check_vma=False,
    )
```

```python
import jax
import jax.numpy as jnp
from jax import lax
from jax.experimental import pallas as pl
from jax.experimental.pallas import tpu as pltpu
from jax.sharding import PartitionSpec as P

MESH = pl.DeviceIdType.MESH
f32 = jnp.float32
bf16 = jnp.bfloat16


def slot_body(factors, occ_energy, vir_energy, i_slot, j_slot, partner_device, pair_count):
    held, virtuals, columns = factors.shape
    pair_slots = i_slot.shape[0]
    occ_count = lax.axis_size("occ")
    capacity = max(2, (3 * pair_slots // 2 + occ_count - 1) // occ_count)
    slot_total = occ_count * capacity
    device_index = lax.axis_index("occ")
    pair_order = jnp.arange(pair_slots, dtype=jnp.int32)
    living = pair_order < pair_count[0]
    target = partner_device[:, 0]
    earlier = (
        (target[:, None] == target[None, :])
        & living[None, :]
        & (pair_order[None, :] < pair_order[:, None])
    )
    slot_rank = jnp.sum(earlier.astype(jnp.int32), axis=1)
    slot_index = target * capacity + slot_rank
    slot_hit = (slot_index[:, None] == jnp.arange(slot_total, dtype=jnp.int32)[None, :]) & living[
        :, None
    ]
    requests = jnp.sum(jnp.where(slot_hit, j_slot[:, None] + 1, 0), axis=0) - 1
    wanted = lax.all_to_all(requests, "occ", split_axis=0, concat_axis=0, tiled=True)
    wanted_hit = (wanted[:, None] == jnp.arange(held, dtype=jnp.int32)[None, :]).astype(
        jnp.bfloat16
    )
    far_index = target * held + j_slot
    piece = lax.all_gather(factors, "occ", axis=0, tiled=True)
    count = piece.shape[0]
    hit = (far_index[:, None] == jnp.arange(count, dtype=jnp.int32)[None, :]).astype(jnp.bfloat16)
    gathered = jnp.dot(
        hit, piece.reshape(count, virtuals * columns), preferred_element_type=jnp.float32
    )
    partner_blocks = gathered.astype(jnp.bfloat16).reshape(pair_slots, virtuals, columns)
    own_blocks = factors[i_slot]
    orbitals = occ_energy.shape[0]
    table = jnp.arange(orbitals, dtype=jnp.int32)
    own_index = device_index * held + i_slot
    energy_own = jnp.sum(
        jnp.where(own_index[:, None] == table[None, :], occ_energy[None, :], 0.0), axis=1
    )
    energy_far = jnp.sum(
        jnp.where(far_index[:, None] == table[None, :], occ_energy[None, :], 0.0), axis=1
    )
    denominator = (
        vir_energy[None, :, None]
        + vir_energy[None, None, :]
        - energy_own[:, None, None]
        - energy_far[:, None, None]
    )
    partial_value = jnp.einsum(
        "pvq,pwq->pvw", own_blocks, partner_blocks, preferred_element_type=jnp.float32
    )
    summed = lax.psum(partial_value, "aux")
    amplitude = jnp.where(living[:, None, None], summed / denominator, 0.0).astype(jnp.bfloat16)
    local_terms = jnp.einsum(
        "pvw,pwq->pvq", amplitude, partner_blocks, preferred_element_type=jnp.float32
    )
    owner_hit = (i_slot[:, None] == jnp.arange(held, dtype=jnp.int32)[None, :]).astype(jnp.float32)
    gamma_local = jnp.einsum("po,pvq->ovq", owner_hit, local_terms, precision=lax.Precision.HIGHEST)
    return_terms = jnp.einsum(
        "pwv,pwq->pvq", amplitude, own_blocks, preferred_element_type=jnp.float32
    ).astype(jnp.bfloat16)
    placed = jnp.dot(
        slot_hit.astype(jnp.bfloat16).T,
        return_terms.reshape(pair_slots, virtuals * columns),
        preferred_element_type=jnp.float32,
    )
    placed = placed.astype(jnp.bfloat16).reshape(slot_total, virtuals, columns)
    returned = lax.all_to_all(placed, "occ", split_axis=0, concat_axis=0, tiled=True)
    gathered_back = jnp.dot(
        wanted_hit.T,
        returned.reshape(slot_total, virtuals * columns),
        preferred_element_type=jnp.float32,
    )
    gamma = gamma_local + gathered_back.reshape(held, virtuals, columns)
    rounded = gamma.astype(jnp.bfloat16)
    stacked = jnp.stack([rounded, factors])
    gamma_rows = rounded.reshape(held * virtuals, columns)
    factor_flat = factors.reshape(held * virtuals, columns)
    piece = lax.all_gather(stacked, "aux", axis=3, tiled=True)
    width_here = piece.shape[3]
    gamma_piece = piece[0].reshape(held * virtuals, width_here)
    factor_piece = piece[1].reshape(held * virtuals, width_here)
    first = jnp.dot(gamma_rows.T, factor_piece, preferred_element_type=jnp.float32)
    second = jnp.dot(factor_flat.T, gamma_piece, preferred_element_type=jnp.float32)
    terms = first + second
    shared = lax.psum_scatter(terms, "occ", scatter_dimension=1, tiled=True)
    factor_scale = float(orbitals * virtuals) ** (-0.5)
    return (gamma, shared * factor_scale)


def nt(a, b):
    return lax.dot_general(a, b, (((1,), (1,)), ((), ())), preferred_element_type=f32)


def tn(a, b):
    return lax.dot_general(a, b, (((0,), (0,)), ((), ())), preferred_element_type=f32)


def kernel(
    f_ref, cnt_ref, e_ref, vcol_ref, vrow_ref,
    gamma_ref, aux_ref,
    kbuf, lbuf, kh, cnt, gacc, gsend, grecv, gfull, gsib, asend, arecv, tsend, trecv,
    ky_s, ky_r, ksib_s, ksib_r, z_s, z_r, x_s, x_r, s_s, s_r,
    cnt_s, cnt_r, g_s, g_r, gs_s, gs_r, a_s, a_r, t_s, t_r,
):
    occ_count = lax.axis_size("occ")
    lines = occ_count // 2
    held, virtuals, width = f_ref.shape
    half = virtuals // 2
    o = lax.axis_index("occ")
    a = lax.axis_index("aux")
    z, x = o // 2, o % 2
    y, c = a // 2, a % 2
    oy, oc, ox = 1 - y, 1 - c, 1 - x

    def dev(occ, aux):
        return {"occ": occ, "aux": aux}

    y_peer, sibling = dev(o, oy * 2 + c), dev(o, y * 2 + oc)
    x_peer = dev(z * 2 + ox, a)

    def rcopy(src, dst, ss, rs, target):
        return pltpu.make_async_remote_copy(
            src_ref=src, dst_ref=dst, send_sem=ss, recv_sem=rs, device_id=target, device_id_type=MESH
        )

    barrier = pltpu.get_barrier_semaphore()
    for s in range(1, occ_count):
        pl.semaphore_signal(barrier, inc=1, device_id=dev((o + s) % occ_count, a), device_id_type=MESH)
    pl.semaphore_signal(barrier, inc=1, device_id=y_peer, device_id_type=MESH)
    pl.semaphore_signal(barrier, inc=1, device_id=sibling, device_id_type=MESH)
    ta = o // 2
    for h in range(2):
        @pl.when(jnp.logical_or(ta != a, o != 2 * a + h))
        def _():
            pl.semaphore_signal(barrier, inc=1, device_id=dev(2 * a + h, ta), device_id_type=MESH)
    pl.semaphore_wait(barrier, occ_count + 1 + jnp.where(ta != a, 2, 1))

    def ky(r):
        return rcopy(f_ref.at[r], kbuf.at[c, y, r], ky_s.at[r], ky_r.at[r], y_peer)

    def ky_wait(r):
        rcopy(f_ref.at[r], kbuf.at[c, oy, r], ky_s.at[r], ky_r.at[r], y_peer).wait_recv()

    def ksib(n, yy, r):
        return rcopy(kbuf.at[c, yy, r], kbuf.at[c, yy, r], ksib_s.at[n], ksib_r.at[n], sibling)

    def ksib_wait(n, yy, r):
        rcopy(kbuf.at[oc, yy, r], kbuf.at[oc, yy, r], ksib_s.at[n], ksib_r.at[n], sibling).wait_recv()

    def item(oo, yy):
        return lbuf.at[oo, c, yy]

    def z_copy(d, zz, yy):
        oo = zz * 2 + x
        return rcopy(item(oo, yy), item(oo, yy), z_s.at[d, zz, yy], z_r.at[zz, yy], dev((z + 1 - 2 * d) * 2 + x, a))

    def x_copy(zz, yy):
        oo = zz * 2 + x
        return rcopy(item(oo, yy), item(oo, yy), x_s.at[zz, yy], x_r.at[zz, yy], x_peer)

    def x_wait(zz, yy):
        oo = zz * 2 + ox
        rcopy(item(oo, yy), item(oo, yy), x_s.at[zz, yy], x_r.at[zz, yy], x_peer).wait_recv()

    def s_copy(oo, yy):
        return rcopy(item(oo, yy), item(oo, yy), s_s.at[oo, yy], s_r.at[oo, yy], sibling)

    def s_wait(oo, yy):
        there = lbuf.at[oo, oc, yy]
        rcopy(there, there, s_s.at[oo, yy], s_r.at[oo, yy], sibling).wait_recv()

    def forward(zz, yy, right, left):
        @pl.when(jnp.logical_and(right, z + 1 < lines))
        def _():
            z_copy(0, zz, yy).start()

        @pl.when(jnp.logical_and(left, z > 0))
        def _():
            z_copy(1, zz, yy).start()

        x_copy(zz, yy).start()
        s_copy(zz * 2 + x, yy).start()

    ky(oy).start()
    lbuf[o, c, y] = f_ref[y]
    forward(z, y, True, True)
    ky(y).start()
    kbuf[c, y] = f_ref[...]
    ksib(0, y, 0).start()
    ksib(1, y, 1).start()
    cnt[o] = cnt_ref[...]

    def cnt_copy(oo):
        return rcopy(cnt_ref, cnt.at[o], cnt_s.at[oo], cnt_r.at[o], dev(oo, a))

    for s in range(1, occ_count):
        cnt_copy((o + s) % occ_count).start()

    ky_wait(y)
    lbuf[o, c, oy] = kbuf[c, oy, y]
    forward(z, oy, True, True)
    ksib(2, oy, y).start()
    ky_wait(oy)
    ksib(3, oy, oy).start()

    gacc[...] = jnp.zeros_like(gacc)
    for s in range(1, occ_count):
        oo = (o + s) % occ_count
        rcopy(cnt_ref, cnt.at[oo], cnt_s.at[oo], cnt_r.at[oo], dev(oo, a)).wait_recv()
    ksib_wait(0, y, 0)
    ksib_wait(1, y, 1)
    ksib_wait(2, oy, y)
    ksib_wait(3, oy, oy)
    for cc in range(2):
        for yy in range(2):
            for k in range(2):
                kh[cc, yy, k * half:(k + 1) * half] = kbuf[cc, yy, k, pl.ds(c * half, half)]
    vhalf = vcol_ref[pl.ds(c * half, half)]
    side = jnp.concatenate([vhalf - e_ref[2 * o], vhalf - e_ref[2 * o + 1]], axis=0)
    vrow = vrow_ref[...]
    rows8 = lax.broadcasted_iota(jnp.int32, cnt_ref.shape, 0)
    lanes8 = lax.broadcasted_iota(jnp.int32, cnt_ref.shape, 1)

    def pick(tile, row, lane):
        here = jnp.logical_and(rows8 == row, lanes8 == lane)
        return jnp.sum(jnp.where(here, tile, 0.0), keepdims=True)

    def work(oo):
        far = 2 * oo + y
        inter = nt(kh[0, 0], lbuf[oo, 0, 0])
        inter += nt(kh[0, 1], lbuf[oo, 0, 1])
        inter += nt(kh[1, 0], lbuf[oo, 1, 0])
        inter += nt(kh[1, 1], lbuf[oo, 1, 1])
        amplitude = (inter / (side + (vrow - e_ref[far]))).astype(bf16)
        mine, theirs = cnt[o], cnt[oo]
        w1 = [pick(mine, k, far) for k in range(2)]
        w2 = [pick(theirs, y, 2 * o + k) for k in range(2)]
        for cc in range(2):
            for yy in range(2):
                term = jnp.dot(amplitude, lbuf[oo, cc, yy], preferred_element_type=f32)
                for k in range(2):
                    part = term[k * half:(k + 1) * half]
                    gacc[cc, yy, k * half:(k + 1) * half] += (
                        w1[k] * part + w2[k] * part.astype(bf16).astype(f32)
                    )

    def place(d, sign):
        zz = z - d + 2 * d * sign
        ok = jnp.logical_and(jnp.logical_and(zz >= 0, zz < lines), jnp.logical_or(d > 0, sign == 0))
        return zz, ok

    def step(d, carry):
        @pl.when(d < lines)
        def _():
            for n in range(2):
                yy = (y + n) % 2
                for sign in range(2):
                    zz, ok = place(d, sign)

                    @pl.when(ok)
                    def _():
                        z_copy(0, zz, yy).wait_recv()
                        forward(zz, yy, sign == 0, sign == 1)

        before = d - 1
        for sign in range(2):
            zz, ok = place(before, sign)

            @pl.when(ok)
            def _():
                for n in range(2):
                    yy = (y + n) % 2
                    x_wait(zz, yy)
                    s_copy(zz * 2 + ox, yy).start()

        def each(n, carry):
            zz, ok = place(before, n // 2)
            oo = zz * 2 + (x + n) % 2

            @pl.when(ok)
            def _():
                s_wait(oo, 0)
                s_wait(oo, 1)
                work(oo)

            return carry

        lax.fori_loop(0, 4, each, 0)
        return carry

    lax.fori_loop(1, lines + 1, step, 0)

    out_width = aux_ref.shape[1]

    def cols(h):
        return slice(h * out_width, (h + 1) * out_width)

    def g_copy(h, cc):
        return rcopy(gsend.at[h, cc], grecv.at[h, cc], g_s.at[h, cc], g_r.at[h, cc], y_peer)

    def gs_copy(h):
        return rcopy(gfull.at[h], gsib.at[h], gs_s.at[h], gs_r.at[h], sibling)

    def a_copy(h, oo):
        return rcopy(asend.at[h, oo], arecv.at[h, o], a_s.at[h, oo], a_r.at[h, o], dev(oo, a))

    def t_copy(h):
        return rcopy(tsend.at[h], trecv.at[o % 2], t_s.at[h], t_r.at[o % 2], dev(2 * a + h, ta))

    def t_far(h):
        return jnp.logical_or(ta != a, o != 2 * a + h)

    for h in range(2):
        for n in range(2):
            cc = (c + 1 + n) % 2
            gsend[h, cc] = gacc[cc, oy][:, cols(h)].astype(bf16)
            g_copy(h, cc).start()

    for h in range(2):
        g_copy(h, oc).wait_recv()
        gfull[h] = gacc[oc, y][:, cols(h)] + grecv[h, oc].astype(f32)
        gs_copy(h).start()
        g_copy(h, c).wait_recv()
        mine = gacc[c, y][:, cols(h)] + grecv[h, c].astype(f32)
        for k in range(2):
            gamma_ref[k, pl.ds(c * half, half), cols(h)] = mine[k * half:(k + 1) * half]
        gs_copy(h).wait_recv()
        for k in range(2):
            gamma_ref[k, pl.ds(oc * half, half), cols(h)] = gsib[h, k * half:(k + 1) * half]
        rounded = gamma_ref[:, :, cols(h)].reshape(held * virtuals, out_width).astype(bf16)

        for n in range(4):
            block = (ta + 2 + n) % 4
            terms = tn(rounded, kbuf[block % 2, block // 2].reshape(held * virtuals, width))
            for g in range(2):
                oo = 2 * block + g
                part = terms[:, cols(g)]
                asend[h, oo] = part.astype(bf16)

                @pl.when(oo == o)
                def _():
                    aux_ref[cols(h)] = part

                @pl.when(oo != o)
                def _():
                    a_copy(h, oo).start()

    for h in range(2):
        total = aux_ref[cols(h)]
        for s in range(1, occ_count):
            oo = (o + s) % occ_count
            rcopy(asend.at[h, oo], arecv.at[h, oo], a_s.at[h, oo], a_r.at[h, oo], dev(oo, a)).wait_recv()
            total += arecv[h, oo].astype(f32)
        tsend[h] = total

        @pl.when(t_far(h))
        def _():
            t_copy(h).start()

        @pl.when(jnp.logical_not(t_far(h)))
        def _():
            trecv[o % 2] = tsend[h]

    scale = float(occ_count * held * virtuals) ** (-0.5)
    for h in range(2):
        @pl.when(t_far(h))
        def _():
            rcopy(tsend.at[h], trecv.at[h], t_s.at[h], t_r.at[h], dev(2 * a + h, ta)).wait_recv()

        aux_ref[cols(h)] = (tsend[h] + trecv[h].T) * scale

    for r in range(2):
        ky(r).wait_send()
        g_copy(r, 0).wait_send()
        g_copy(r, 1).wait_send()
        gs_copy(r).wait_send()
    ksib(0, y, 0).wait_send()
    ksib(1, y, 1).wait_send()
    ksib(2, oy, y).wait_send()
    ksib(3, oy, oy).wait_send()
    for s in range(1, occ_count):
        oo = (o + s) % occ_count
        cnt_copy(oo).wait_send()
        a_copy(0, oo).wait_send()
        a_copy(1, oo).wait_send()
    for h in range(2):
        @pl.when(t_far(h))
        def _():
            t_copy(h).wait_send()

    def drain(zz, carry):
        for yy in range(2):
            @pl.when(jnp.logical_and(zz <= z, z + 1 < lines))
            def _():
                z_copy(0, zz, yy).wait_send()

            @pl.when(jnp.logical_and(zz >= z, z > 0))
            def _():
                z_copy(1, zz, yy).wait_send()

            x_copy(zz, yy).wait_send()
            s_copy(zz * 2, yy).wait_send()
            s_copy(zz * 2 + 1, yy).wait_send()
        return carry

    lax.fori_loop(0, lines, drain, 0)


def table_body(factors, occ_energy, vir_energy, i_slot, j_slot, partner_device, pair_count):
    held, virtuals, width = factors.shape
    slots = i_slot.shape[0]
    occ_count = lax.axis_size("occ")
    lines = occ_count // 2
    out_width = 4 * width // occ_count
    living = jnp.arange(slots, dtype=jnp.int32) < pair_count[0]
    far = partner_device[:, 0] * held + j_slot
    row_hit = jnp.logical_and(
        i_slot[None, :, None] == jnp.arange(8, dtype=jnp.int32)[:, None, None], living[None, :, None]
    )
    col_hit = far[None, :, None] == jnp.arange(128, dtype=jnp.int32)[None, None, :]
    counts = jnp.sum(jnp.logical_and(row_hit, col_hit).astype(f32), axis=1)
    vmem = pl.BlockSpec(memory_space=pltpu.VMEM)
    dma = pltpu.SemaphoreType.DMA
    return pl.pallas_call(
        kernel,
        out_shape=(
            jax.ShapeDtypeStruct((held, virtuals, width), f32),
            jax.ShapeDtypeStruct((width, out_width), f32),
        ),
        in_specs=[vmem, vmem, pl.BlockSpec(memory_space=pltpu.SMEM), vmem, vmem],
        out_specs=(vmem, vmem),
        scratch_shapes=[
            pltpu.VMEM((2, 2, held, virtuals, width), bf16),
            pltpu.VMEM((occ_count, 2, 2, virtuals, width), bf16),
            pltpu.VMEM((2, 2, virtuals, width), bf16),
            pltpu.VMEM((occ_count, 8, 128), f32),
            pltpu.VMEM((2, 2, virtuals, width), f32),
            pltpu.VMEM((2, 2, virtuals, out_width), bf16),
            pltpu.VMEM((2, 2, virtuals, out_width), bf16),
            pltpu.VMEM((2, virtuals, out_width), f32),
            pltpu.VMEM((2, virtuals, out_width), f32),
            pltpu.VMEM((2, occ_count, out_width, out_width), bf16),
            pltpu.VMEM((2, occ_count, out_width, out_width), bf16),
            pltpu.VMEM((2, out_width, out_width), f32),
            pltpu.VMEM((2, out_width, out_width), f32),
            dma((2,)), dma((2,)), dma((4,)), dma((4,)),
            dma((2, lines, 2)), dma((lines, 2)), dma((lines, 2)), dma((lines, 2)),
            dma((occ_count, 2)), dma((occ_count, 2)),
            dma((occ_count,)), dma((occ_count,)), dma((2, 2)), dma((2, 2)), dma((2,)), dma((2,)),
            dma((2, occ_count)), dma((2, occ_count)), dma((2,)), dma((2,)),
        ],
        compiler_params=pltpu.CompilerParams(
            collective_id=0, has_side_effects=True, vmem_limit_bytes=40 * 1024 * 1024
        ),
    )(factors, counts, occ_energy, vir_energy[:, None], vir_energy[None, :])


def body(*operands):
    factors, i_slot = operands[0], operands[3]
    held, virtuals, width = factors.shape
    occ_count, aux_count = lax.axis_size("occ"), lax.axis_size("aux")
    orbitals = held * occ_count
    fits = (
        held == 2 and aux_count == 4 and occ_count == 2 * aux_count and orbitals <= 128
        and orbitals * orbitals <= occ_count * i_slot.shape[0]
        and virtuals == width and width % 256 == 0 and 4 * width == occ_count * 128
    )
    return table_body(*operands) if fits else slot_body(*operands)


def solution(mesh):
    placed = (P("occ", None, "aux"), P(), P(), P("occ"), P("occ"), P("occ", None), P("occ"))
    return jax.shard_map(
        body,
        mesh=mesh,
        in_specs=placed,
        out_specs=(P("occ", None, "aux"), P("aux", "occ")),
        check_vma=False,
    )
```

```python
import jax
import jax.numpy as jnp
from jax import lax
from jax.experimental import pallas as pl
from jax.experimental.pallas import tpu as pltpu
from jax.sharding import PartitionSpec as P

MESH = pl.DeviceIdType.MESH
f32 = jnp.float32
bf16 = jnp.bfloat16


def slot_body(factors, occ_energy, vir_energy, i_slot, j_slot, partner_device, pair_count):
    held, virtuals, columns = factors.shape
    pair_slots = i_slot.shape[0]
    occ_count = lax.axis_size("occ")
    capacity = max(2, (3 * pair_slots // 2 + occ_count - 1) // occ_count)
    slot_total = occ_count * capacity
    device_index = lax.axis_index("occ")
    pair_order = jnp.arange(pair_slots, dtype=jnp.int32)
    living = pair_order < pair_count[0]
    target = partner_device[:, 0]
    earlier = (
        (target[:, None] == target[None, :])
        & living[None, :]
        & (pair_order[None, :] < pair_order[:, None])
    )
    slot_rank = jnp.sum(earlier.astype(jnp.int32), axis=1)
    slot_index = target * capacity + slot_rank
    slot_hit = (slot_index[:, None] == jnp.arange(slot_total, dtype=jnp.int32)[None, :]) & living[
        :, None
    ]
    requests = jnp.sum(jnp.where(slot_hit, j_slot[:, None] + 1, 0), axis=0) - 1
    wanted = lax.all_to_all(requests, "occ", split_axis=0, concat_axis=0, tiled=True)
    wanted_hit = (wanted[:, None] == jnp.arange(held, dtype=jnp.int32)[None, :]).astype(
        jnp.bfloat16
    )
    far_index = target * held + j_slot
    piece = lax.all_gather(factors, "occ", axis=0, tiled=True)
    count = piece.shape[0]
    hit = (far_index[:, None] == jnp.arange(count, dtype=jnp.int32)[None, :]).astype(jnp.bfloat16)
    gathered = jnp.dot(
        hit, piece.reshape(count, virtuals * columns), preferred_element_type=jnp.float32
    )
    partner_blocks = gathered.astype(jnp.bfloat16).reshape(pair_slots, virtuals, columns)
    own_blocks = factors[i_slot]
    orbitals = occ_energy.shape[0]
    table = jnp.arange(orbitals, dtype=jnp.int32)
    own_index = device_index * held + i_slot
    energy_own = jnp.sum(
        jnp.where(own_index[:, None] == table[None, :], occ_energy[None, :], 0.0), axis=1
    )
    energy_far = jnp.sum(
        jnp.where(far_index[:, None] == table[None, :], occ_energy[None, :], 0.0), axis=1
    )
    denominator = (
        vir_energy[None, :, None]
        + vir_energy[None, None, :]
        - energy_own[:, None, None]
        - energy_far[:, None, None]
    )
    partial_value = jnp.einsum(
        "pvq,pwq->pvw", own_blocks, partner_blocks, preferred_element_type=jnp.float32
    )
    summed = lax.psum(partial_value, "aux")
    amplitude = jnp.where(living[:, None, None], summed / denominator, 0.0).astype(jnp.bfloat16)
    local_terms = jnp.einsum(
        "pvw,pwq->pvq", amplitude, partner_blocks, preferred_element_type=jnp.float32
    )
    owner_hit = (i_slot[:, None] == jnp.arange(held, dtype=jnp.int32)[None, :]).astype(jnp.float32)
    gamma_local = jnp.einsum("po,pvq->ovq", owner_hit, local_terms, precision=lax.Precision.HIGHEST)
    return_terms = jnp.einsum(
        "pwv,pwq->pvq", amplitude, own_blocks, preferred_element_type=jnp.float32
    ).astype(jnp.bfloat16)
    placed = jnp.dot(
        slot_hit.astype(jnp.bfloat16).T,
        return_terms.reshape(pair_slots, virtuals * columns),
        preferred_element_type=jnp.float32,
    )
    placed = placed.astype(jnp.bfloat16).reshape(slot_total, virtuals, columns)
    returned = lax.all_to_all(placed, "occ", split_axis=0, concat_axis=0, tiled=True)
    gathered_back = jnp.dot(
        wanted_hit.T,
        returned.reshape(slot_total, virtuals * columns),
        preferred_element_type=jnp.float32,
    )
    gamma = gamma_local + gathered_back.reshape(held, virtuals, columns)
    rounded = gamma.astype(jnp.bfloat16)
    stacked = jnp.stack([rounded, factors])
    gamma_rows = rounded.reshape(held * virtuals, columns)
    factor_flat = factors.reshape(held * virtuals, columns)
    piece = lax.all_gather(stacked, "aux", axis=3, tiled=True)
    width_here = piece.shape[3]
    gamma_piece = piece[0].reshape(held * virtuals, width_here)
    factor_piece = piece[1].reshape(held * virtuals, width_here)
    first = jnp.dot(gamma_rows.T, factor_piece, preferred_element_type=jnp.float32)
    second = jnp.dot(factor_flat.T, gamma_piece, preferred_element_type=jnp.float32)
    terms = first + second
    shared = lax.psum_scatter(terms, "occ", scatter_dimension=1, tiled=True)
    factor_scale = float(orbitals * virtuals) ** (-0.5)
    return (gamma, shared * factor_scale)


def nt(a, b):
    return lax.dot_general(a, b, (((1,), (1,)), ((), ())), preferred_element_type=f32)


def tn(a, b):
    return lax.dot_general(a, b, (((0,), (0,)), ((), ())), preferred_element_type=f32)


def kernel(
    f_hbm, e_hbm, v_hbm, i_hbm, j_hbm, partner_hbm, count_ref,
    gamma_ref, aux_ref,
    kbuf, lbuf, kh, cnt, gacc, gsend, grecv, gfull, gsib, asend, arecv, tsend, trecv,
    ky_s, ky_r, ksib_s, ksib_r, z_s, z_r, x_s, x_r, s_s, s_r,
    cnt_s, cnt_r, g_s, g_r, gs_s, gs_r, a_s, a_r, t_s, t_r,
    f_ref, e_ref, v_ref, i_ref, j_ref, partner_ref, cnt_ref, side, in_s,
):
    occ_count = lax.axis_size("occ")
    lines = occ_count // 2
    held, virtuals, width = f_ref.shape
    half = virtuals // 2
    o = lax.axis_index("occ")
    a = lax.axis_index("aux")
    z, x = o // 2, o % 2
    y, c = a // 2, a % 2
    oy, oc, ox = 1 - y, 1 - c, 1 - x

    def dev(occ, aux):
        return {"occ": occ, "aux": aux}

    y_peer, sibling = dev(o, oy * 2 + c), dev(o, y * 2 + oc)
    x_peer = dev(z * 2 + ox, a)

    def rcopy(src, dst, ss, rs, target):
        return pltpu.make_async_remote_copy(
            src_ref=src, dst_ref=dst, send_sem=ss, recv_sem=rs, device_id=target, device_id_type=MESH
        )

    pairs = (
        (f_hbm, f_ref), (e_hbm, e_ref), (v_hbm, v_ref), (i_hbm, i_ref), (j_hbm, j_ref),
        (partner_hbm, partner_ref),
    )
    loads = [pltpu.make_async_copy(there, here, in_s.at[n]) for n, (there, here) in enumerate(pairs)]
    for load in loads:
        load.start()

    barrier = pltpu.get_barrier_semaphore()
    for s in range(1, occ_count):
        pl.semaphore_signal(barrier, inc=1, device_id=dev((o + s) % occ_count, a), device_id_type=MESH)
    pl.semaphore_signal(barrier, inc=1, device_id=y_peer, device_id_type=MESH)
    pl.semaphore_signal(barrier, inc=1, device_id=sibling, device_id_type=MESH)
    ta = o // 2
    for h in range(2):
        @pl.when(jnp.logical_or(ta != a, o != 2 * a + h))
        def _():
            pl.semaphore_signal(barrier, inc=1, device_id=dev(2 * a + h, ta), device_id_type=MESH)
    pl.semaphore_wait(barrier, occ_count + 1 + jnp.where(ta != a, 2, 1))

    def ky(r):
        return rcopy(f_ref.at[r], kbuf.at[c, y, r], ky_s.at[r], ky_r.at[r], y_peer)

    def ky_wait(r):
        rcopy(f_ref.at[r], kbuf.at[c, oy, r], ky_s.at[r], ky_r.at[r], y_peer).wait_recv()

    def ksib(n, yy, r):
        return rcopy(kbuf.at[c, yy, r], kbuf.at[c, yy, r], ksib_s.at[n], ksib_r.at[n], sibling)

    def ksib_wait(n, yy, r):
        rcopy(kbuf.at[oc, yy, r], kbuf.at[oc, yy, r], ksib_s.at[n], ksib_r.at[n], sibling).wait_recv()

    def item(oo, yy):
        return lbuf.at[oo, c, yy]

    def z_copy(d, zz, yy):
        oo = zz * 2 + x
        return rcopy(item(oo, yy), item(oo, yy), z_s.at[d, zz, yy], z_r.at[zz, yy], dev((z + 1 - 2 * d) * 2 + x, a))

    def x_copy(zz, yy):
        oo = zz * 2 + x
        return rcopy(item(oo, yy), item(oo, yy), x_s.at[zz, yy], x_r.at[zz, yy], x_peer)

    def x_wait(zz, yy):
        oo = zz * 2 + ox
        rcopy(item(oo, yy), item(oo, yy), x_s.at[zz, yy], x_r.at[zz, yy], x_peer).wait_recv()

    def s_copy(oo, yy):
        return rcopy(item(oo, yy), item(oo, yy), s_s.at[oo, yy], s_r.at[oo, yy], sibling)

    def s_wait(oo, yy):
        there = lbuf.at[oo, oc, yy]
        rcopy(there, there, s_s.at[oo, yy], s_r.at[oo, yy], sibling).wait_recv()

    def forward(zz, yy, right, left):
        @pl.when(jnp.logical_and(right, z + 1 < lines))
        def _():
            z_copy(0, zz, yy).start()

        @pl.when(jnp.logical_and(left, z > 0))
        def _():
            z_copy(1, zz, yy).start()

        x_copy(zz, yy).start()
        s_copy(zz * 2 + x, yy).start()

    loads[0].wait()
    ky(oy).start()
    lbuf[o, c, y] = f_ref[y]
    forward(z, y, True, True)
    ky(y).start()
    kbuf[c, y] = f_ref[...]
    ksib(0, y, 0).start()
    ksib(1, y, 1).start()
    for load in loads[1:]:
        load.wait()

    slots = i_ref.shape[1]
    order = lax.broadcasted_iota(jnp.int32, (8, slots), 1)
    row_hit = jnp.logical_and(
        i_ref[...] == lax.broadcasted_iota(jnp.int32, (8, slots), 0), order < count_ref[0]
    )
    col_hit = partner_ref[...] * held + j_ref[...] == lax.broadcasted_iota(jnp.int32, (128, slots), 0)
    cnt_ref[...] = nt(row_hit.astype(f32).astype(bf16), col_hit.astype(f32).astype(bf16))
    cnt[o] = cnt_ref[...]

    def cnt_copy(oo):
        return rcopy(cnt_ref, cnt.at[o], cnt_s.at[oo], cnt_r.at[o], dev(oo, a))

    for s in range(1, occ_count):
        cnt_copy((o + s) % occ_count).start()

    ky_wait(y)
    lbuf[o, c, oy] = kbuf[c, oy, y]
    forward(z, oy, True, True)
    ksib(2, oy, y).start()
    ky_wait(oy)
    ksib(3, oy, oy).start()

    gacc[...] = jnp.zeros_like(gacc)
    for s in range(1, occ_count):
        oo = (o + s) % occ_count
        rcopy(cnt_ref, cnt.at[oo], cnt_s.at[oo], cnt_r.at[oo], dev(oo, a)).wait_recv()
    ksib_wait(0, y, 0)
    ksib_wait(1, y, 1)
    ksib_wait(2, oy, y)
    ksib_wait(3, oy, oy)
    for cc in range(2):
        for yy in range(2):
            for k in range(2):
                kh[cc, yy, k * half:(k + 1) * half] = kbuf[cc, yy, k, pl.ds(c * half, half)]
    column = jnp.broadcast_to(v_ref[:, pl.ds(pl.multiple_of(c * half, half), half)], (width, half)).T
    side[0:half] = column - e_ref[0, 2 * o]
    side[half:virtuals] = column - e_ref[0, 2 * o + 1]
    vrow = v_ref[...]
    rows8 = lax.broadcasted_iota(jnp.int32, cnt_ref.shape, 0)
    lanes8 = lax.broadcasted_iota(jnp.int32, cnt_ref.shape, 1)

    def pick(tile, row, lane):
        here = jnp.logical_and(rows8 == row, lanes8 == lane)
        return jnp.sum(jnp.where(here, tile, 0.0), keepdims=True)

    def work(oo):
        far = 2 * oo + y
        inter = nt(kh[0, 0], lbuf[oo, 0, 0])
        inter += nt(kh[0, 1], lbuf[oo, 0, 1])
        inter += nt(kh[1, 0], lbuf[oo, 1, 0])
        inter += nt(kh[1, 1], lbuf[oo, 1, 1])
        amplitude = (inter / (side[...] + (vrow - e_ref[0, far]))).astype(bf16)
        mine, theirs = cnt[o], cnt[oo]
        w1 = [pick(mine, k, far) for k in range(2)]
        w2 = [pick(theirs, y, 2 * o + k) for k in range(2)]
        for cc in range(2):
            for yy in range(2):
                term = jnp.dot(amplitude, lbuf[oo, cc, yy], preferred_element_type=f32)
                for k in range(2):
                    part = term[k * half:(k + 1) * half]
                    gacc[cc, yy, k * half:(k + 1) * half] += (
                        w1[k] * part + w2[k] * part.astype(bf16).astype(f32)
                    )

    def place(d, sign):
        zz = z - d + 2 * d * sign
        ok = jnp.logical_and(jnp.logical_and(zz >= 0, zz < lines), jnp.logical_or(d > 0, sign == 0))
        return zz, ok

    def step(d, carry):
        @pl.when(d < lines)
        def _():
            for n in range(2):
                yy = (y + n) % 2
                for sign in range(2):
                    zz, ok = place(d, sign)

                    @pl.when(ok)
                    def _():
                        z_copy(0, zz, yy).wait_recv()
                        forward(zz, yy, sign == 0, sign == 1)

        before = d - 1
        for sign in range(2):
            zz, ok = place(before, sign)

            @pl.when(ok)
            def _():
                for n in range(2):
                    yy = (y + n) % 2
                    x_wait(zz, yy)
                    s_copy(zz * 2 + ox, yy).start()

        def each(n, carry):
            zz, ok = place(before, n // 2)
            oo = zz * 2 + (x + n) % 2

            @pl.when(ok)
            def _():
                s_wait(oo, 0)
                s_wait(oo, 1)
                work(oo)

            return carry

        lax.fori_loop(0, 4, each, 0)
        return carry

    lax.fori_loop(1, lines + 1, step, 0)

    out_width = aux_ref.shape[1]

    def cols(h):
        return slice(h * out_width, (h + 1) * out_width)

    def g_copy(h, cc):
        return rcopy(gsend.at[h, cc], grecv.at[h, cc], g_s.at[h, cc], g_r.at[h, cc], y_peer)

    def gs_copy(h):
        return rcopy(gfull.at[h], gsib.at[h], gs_s.at[h], gs_r.at[h], sibling)

    def a_copy(h, oo):
        return rcopy(asend.at[h, oo], arecv.at[h, o], a_s.at[h, oo], a_r.at[h, o], dev(oo, a))

    def t_copy(h):
        return rcopy(tsend.at[h], trecv.at[o % 2], t_s.at[h], t_r.at[o % 2], dev(2 * a + h, ta))

    def t_far(h):
        return jnp.logical_or(ta != a, o != 2 * a + h)

    for h in range(2):
        for n in range(2):
            cc = (c + 1 + n) % 2
            gsend[h, cc] = gacc[cc, oy][:, cols(h)].astype(bf16)
            g_copy(h, cc).start()

    for h in range(2):
        g_copy(h, oc).wait_recv()
        gfull[h] = gacc[oc, y][:, cols(h)] + grecv[h, oc].astype(f32)
        gs_copy(h).start()
        g_copy(h, c).wait_recv()
        mine = gacc[c, y][:, cols(h)] + grecv[h, c].astype(f32)
        for k in range(2):
            gamma_ref[k, pl.ds(c * half, half), cols(h)] = mine[k * half:(k + 1) * half]
        gs_copy(h).wait_recv()
        for k in range(2):
            gamma_ref[k, pl.ds(oc * half, half), cols(h)] = gsib[h, k * half:(k + 1) * half]
        rounded = gamma_ref[:, :, cols(h)].reshape(held * virtuals, out_width).astype(bf16)

        for n in range(4):
            block = (ta + 2 + n) % 4
            terms = tn(rounded, kbuf[block % 2, block // 2].reshape(held * virtuals, width))
            for g in range(2):
                oo = 2 * block + g
                part = terms[:, cols(g)]
                asend[h, oo] = part.astype(bf16)

                @pl.when(oo == o)
                def _():
                    aux_ref[cols(h)] = part

                @pl.when(oo != o)
                def _():
                    a_copy(h, oo).start()

    for h in range(2):
        total = aux_ref[cols(h)]
        for s in range(1, occ_count):
            oo = (o + s) % occ_count
            rcopy(asend.at[h, oo], arecv.at[h, oo], a_s.at[h, oo], a_r.at[h, oo], dev(oo, a)).wait_recv()
            total += arecv[h, oo].astype(f32)
        tsend[h] = total

        @pl.when(t_far(h))
        def _():
            t_copy(h).start()

        @pl.when(jnp.logical_not(t_far(h)))
        def _():
            trecv[o % 2] = tsend[h]

    scale = float(occ_count * held * virtuals) ** (-0.5)
    for h in range(2):
        @pl.when(t_far(h))
        def _():
            rcopy(tsend.at[h], trecv.at[h], t_s.at[h], t_r.at[h], dev(2 * a + h, ta)).wait_recv()

        aux_ref[cols(h)] = (tsend[h] + trecv[h].T) * scale

    for r in range(2):
        ky(r).wait_send()
        g_copy(r, 0).wait_send()
        g_copy(r, 1).wait_send()
        gs_copy(r).wait_send()
    ksib(0, y, 0).wait_send()
    ksib(1, y, 1).wait_send()
    ksib(2, oy, y).wait_send()
    ksib(3, oy, oy).wait_send()
    for s in range(1, occ_count):
        oo = (o + s) % occ_count
        cnt_copy(oo).wait_send()
        a_copy(0, oo).wait_send()
        a_copy(1, oo).wait_send()
    for h in range(2):
        @pl.when(t_far(h))
        def _():
            t_copy(h).wait_send()

    def drain(zz, carry):
        for yy in range(2):
            @pl.when(jnp.logical_and(zz <= z, z + 1 < lines))
            def _():
                z_copy(0, zz, yy).wait_send()

            @pl.when(jnp.logical_and(zz >= z, z > 0))
            def _():
                z_copy(1, zz, yy).wait_send()

            x_copy(zz, yy).wait_send()
            s_copy(zz * 2, yy).wait_send()
            s_copy(zz * 2 + 1, yy).wait_send()
        return carry

    lax.fori_loop(0, lines, drain, 0)


def table_body(factors, occ_energy, vir_energy, i_slot, j_slot, partner_device, pair_count):
    held, virtuals, width = factors.shape
    slots = i_slot.shape[0]
    orbitals = occ_energy.shape[0]
    occ_count = lax.axis_size("occ")
    lines = occ_count // 2
    out_width = 4 * width // occ_count
    vmem = pl.BlockSpec(memory_space=pltpu.VMEM)
    dma = pltpu.SemaphoreType.DMA
    return pl.pallas_call(
        kernel,
        out_shape=(
            jax.ShapeDtypeStruct((held, virtuals, width), f32),
            jax.ShapeDtypeStruct((width, out_width), f32),
        ),
        in_specs=[pl.BlockSpec(memory_space=pltpu.HBM)] * 6 + [pl.BlockSpec(memory_space=pltpu.SMEM)],
        out_specs=(vmem, vmem),
        scratch_shapes=[
            pltpu.VMEM((2, 2, held, virtuals, width), bf16),
            pltpu.VMEM((occ_count, 2, 2, virtuals, width), bf16),
            pltpu.VMEM((2, 2, virtuals, width), bf16),
            pltpu.VMEM((occ_count, 8, 128), f32),
            pltpu.VMEM((2, 2, virtuals, width), f32),
            pltpu.VMEM((2, 2, virtuals, out_width), bf16),
            pltpu.VMEM((2, 2, virtuals, out_width), bf16),
            pltpu.VMEM((2, virtuals, out_width), f32),
            pltpu.VMEM((2, virtuals, out_width), f32),
            pltpu.VMEM((2, occ_count, out_width, out_width), bf16),
            pltpu.VMEM((2, occ_count, out_width, out_width), bf16),
            pltpu.VMEM((2, out_width, out_width), f32),
            pltpu.VMEM((2, out_width, out_width), f32),
            dma((2,)), dma((2,)), dma((4,)), dma((4,)),
            dma((2, lines, 2)), dma((lines, 2)), dma((lines, 2)), dma((lines, 2)),
            dma((occ_count, 2)), dma((occ_count, 2)),
            dma((occ_count,)), dma((occ_count,)), dma((2, 2)), dma((2, 2)), dma((2,)), dma((2,)),
            dma((2, occ_count)), dma((2, occ_count)), dma((2,)), dma((2,)),
            pltpu.VMEM((held, virtuals, width), bf16),
            pltpu.SMEM((1, orbitals), f32),
            pltpu.VMEM((1, virtuals), f32),
            pltpu.VMEM((1, slots), jnp.int32),
            pltpu.VMEM((1, slots), jnp.int32),
            pltpu.VMEM((1, slots), jnp.int32),
            pltpu.VMEM((8, 128), f32),
            pltpu.VMEM((virtuals, virtuals), f32),
            dma((6,)),
        ],
        compiler_params=pltpu.CompilerParams(
            collective_id=0, has_side_effects=True, vmem_limit_bytes=64 * 1024 * 1024
        ),
    )(
        factors, occ_energy[None, :], vir_energy[None, :], i_slot[None, :], j_slot[None, :],
        partner_device.reshape(1, slots), pair_count,
    )


def body(*operands):
    factors, i_slot = operands[0], operands[3]
    held, virtuals, width = factors.shape
    occ_count, aux_count = lax.axis_size("occ"), lax.axis_size("aux")
    orbitals = held * occ_count
    fits = (
        held == 2 and aux_count == 4 and occ_count == 2 * aux_count and orbitals <= 128
        and orbitals * orbitals <= occ_count * i_slot.shape[0]
        and virtuals == width and width % 256 == 0 and 4 * width == occ_count * 128
    )
    return table_body(*operands) if fits else slot_body(*operands)


def solution(mesh):
    placed = (P("occ", None, "aux"), P(), P(), P("occ"), P("occ"), P("occ", None), P("occ"))
    return jax.shard_map(
        body,
        mesh=mesh,
        in_specs=placed,
        out_specs=(P("occ", None, "aux"), P("aux", "occ")),
        check_vma=False,
    )
```

```python
import jax
import jax.numpy as jnp
from jax import lax
from jax.experimental import pallas as pl
from jax.experimental.pallas import tpu as pltpu
from jax.sharding import PartitionSpec as P

MESH = pl.DeviceIdType.MESH
f32 = jnp.float32
bf16 = jnp.bfloat16


def slot_body(factors, occ_energy, vir_energy, i_slot, j_slot, partner_device, pair_count):
    held, virtuals, columns = factors.shape
    pair_slots = i_slot.shape[0]
    occ_count = lax.axis_size("occ")
    capacity = max(2, (3 * pair_slots // 2 + occ_count - 1) // occ_count)
    slot_total = occ_count * capacity
    device_index = lax.axis_index("occ")
    pair_order = jnp.arange(pair_slots, dtype=jnp.int32)
    living = pair_order < pair_count[0]
    target = partner_device[:, 0]
    earlier = (
        (target[:, None] == target[None, :])
        & living[None, :]
        & (pair_order[None, :] < pair_order[:, None])
    )
    slot_rank = jnp.sum(earlier.astype(jnp.int32), axis=1)
    slot_index = target * capacity + slot_rank
    slot_hit = (slot_index[:, None] == jnp.arange(slot_total, dtype=jnp.int32)[None, :]) & living[
        :, None
    ]
    requests = jnp.sum(jnp.where(slot_hit, j_slot[:, None] + 1, 0), axis=0) - 1
    wanted = lax.all_to_all(requests, "occ", split_axis=0, concat_axis=0, tiled=True)
    wanted_hit = (wanted[:, None] == jnp.arange(held, dtype=jnp.int32)[None, :]).astype(
        jnp.bfloat16
    )
    far_index = target * held + j_slot
    piece = lax.all_gather(factors, "occ", axis=0, tiled=True)
    count = piece.shape[0]
    hit = (far_index[:, None] == jnp.arange(count, dtype=jnp.int32)[None, :]).astype(jnp.bfloat16)
    gathered = jnp.dot(
        hit, piece.reshape(count, virtuals * columns), preferred_element_type=jnp.float32
    )
    partner_blocks = gathered.astype(jnp.bfloat16).reshape(pair_slots, virtuals, columns)
    own_blocks = factors[i_slot]
    orbitals = occ_energy.shape[0]
    table = jnp.arange(orbitals, dtype=jnp.int32)
    own_index = device_index * held + i_slot
    energy_own = jnp.sum(
        jnp.where(own_index[:, None] == table[None, :], occ_energy[None, :], 0.0), axis=1
    )
    energy_far = jnp.sum(
        jnp.where(far_index[:, None] == table[None, :], occ_energy[None, :], 0.0), axis=1
    )
    denominator = (
        vir_energy[None, :, None]
        + vir_energy[None, None, :]
        - energy_own[:, None, None]
        - energy_far[:, None, None]
    )
    partial_value = jnp.einsum(
        "pvq,pwq->pvw", own_blocks, partner_blocks, preferred_element_type=jnp.float32
    )
    summed = lax.psum(partial_value, "aux")
    amplitude = jnp.where(living[:, None, None], summed / denominator, 0.0).astype(jnp.bfloat16)
    local_terms = jnp.einsum(
        "pvw,pwq->pvq", amplitude, partner_blocks, preferred_element_type=jnp.float32
    )
    owner_hit = (i_slot[:, None] == jnp.arange(held, dtype=jnp.int32)[None, :]).astype(jnp.float32)
    gamma_local = jnp.einsum("po,pvq->ovq", owner_hit, local_terms, precision=lax.Precision.HIGHEST)
    return_terms = jnp.einsum(
        "pwv,pwq->pvq", amplitude, own_blocks, preferred_element_type=jnp.float32
    ).astype(jnp.bfloat16)
    placed = jnp.dot(
        slot_hit.astype(jnp.bfloat16).T,
        return_terms.reshape(pair_slots, virtuals * columns),
        preferred_element_type=jnp.float32,
    )
    placed = placed.astype(jnp.bfloat16).reshape(slot_total, virtuals, columns)
    returned = lax.all_to_all(placed, "occ", split_axis=0, concat_axis=0, tiled=True)
    gathered_back = jnp.dot(
        wanted_hit.T,
        returned.reshape(slot_total, virtuals * columns),
        preferred_element_type=jnp.float32,
    )
    gamma = gamma_local + gathered_back.reshape(held, virtuals, columns)
    rounded = gamma.astype(jnp.bfloat16)
    stacked = jnp.stack([rounded, factors])
    gamma_rows = rounded.reshape(held * virtuals, columns)
    factor_flat = factors.reshape(held * virtuals, columns)
    piece = lax.all_gather(stacked, "aux", axis=3, tiled=True)
    width_here = piece.shape[3]
    gamma_piece = piece[0].reshape(held * virtuals, width_here)
    factor_piece = piece[1].reshape(held * virtuals, width_here)
    first = jnp.dot(gamma_rows.T, factor_piece, preferred_element_type=jnp.float32)
    second = jnp.dot(factor_flat.T, gamma_piece, preferred_element_type=jnp.float32)
    terms = first + second
    shared = lax.psum_scatter(terms, "occ", scatter_dimension=1, tiled=True)
    factor_scale = float(orbitals * virtuals) ** (-0.5)
    return (gamma, shared * factor_scale)


def nt(a, b):
    return lax.dot_general(a, b, (((1,), (1,)), ((), ())), preferred_element_type=f32)


def tn(a, b):
    return lax.dot_general(a, b, (((0,), (0,)), ((), ())), preferred_element_type=f32)


def kernel(
    f_hbm, e_hbm, v_hbm, i_hbm, j_hbm, partner_hbm, count_ref,
    gamma_ref, aux_ref,
    kbuf, lbuf, kh, cnt, gacc, gsend, grecv, gfull, gsib, asend, arecv, tsend, trecv,
    ky_s, ky_r, ksib_s, ksib_r, z_s, z_r, x_s, x_r, s_s, s_r,
    cnt_s, cnt_r, g_s, g_r, gs_s, gs_r, a_s, a_r, t_s, t_r,
    f_ref, e_ref, v_ref, i_ref, j_ref, partner_ref, cnt_ref, side, in_s,
):
    occ_count = lax.axis_size("occ")
    lines = occ_count // 2
    held, virtuals, width = f_ref.shape
    half = virtuals // 2
    o = lax.axis_index("occ")
    a = lax.axis_index("aux")
    z, x = o // 2, o % 2
    y, c = a // 2, a % 2
    oy, oc, ox = 1 - y, 1 - c, 1 - x

    def dev(occ, aux):
        return {"occ": occ, "aux": aux}

    y_peer, sibling = dev(o, oy * 2 + c), dev(o, y * 2 + oc)
    x_peer = dev(z * 2 + ox, a)

    def rcopy(src, dst, ss, rs, target):
        return pltpu.make_async_remote_copy(
            src_ref=src, dst_ref=dst, send_sem=ss, recv_sem=rs, device_id=target, device_id_type=MESH
        )

    pairs = (
        (f_hbm, f_ref), (e_hbm, e_ref), (v_hbm, v_ref), (i_hbm, i_ref), (j_hbm, j_ref),
        (partner_hbm, partner_ref),
    )
    loads = [pltpu.make_async_copy(there, here, in_s.at[n]) for n, (there, here) in enumerate(pairs)]
    for load in loads:
        load.start()

    barrier = pltpu.get_barrier_semaphore()
    for s in range(1, occ_count):
        pl.semaphore_signal(barrier, inc=1, device_id=dev((o + s) % occ_count, a), device_id_type=MESH)
    pl.semaphore_signal(barrier, inc=1, device_id=y_peer, device_id_type=MESH)
    pl.semaphore_signal(barrier, inc=1, device_id=sibling, device_id_type=MESH)
    ta = o // 2
    for h in range(2):
        @pl.when(jnp.logical_or(ta != a, o != 2 * a + h))
        def _():
            pl.semaphore_signal(barrier, inc=1, device_id=dev(2 * a + h, ta), device_id_type=MESH)
    pl.semaphore_wait(barrier, occ_count + 1 + jnp.where(ta != a, 2, 1))

    def ky(r):
        return rcopy(f_ref.at[r], kbuf.at[c, y, r], ky_s.at[r], ky_r.at[r], y_peer)

    def ky_wait(r):
        rcopy(f_ref.at[r], kbuf.at[c, oy, r], ky_s.at[r], ky_r.at[r], y_peer).wait_recv()

    def ksib(n, yy, r):
        return rcopy(kbuf.at[c, yy, r], kbuf.at[c, yy, r], ksib_s.at[n], ksib_r.at[n], sibling)

    def ksib_wait(n, yy, r):
        rcopy(kbuf.at[oc, yy, r], kbuf.at[oc, yy, r], ksib_s.at[n], ksib_r.at[n], sibling).wait_recv()

    def item(oo, yy):
        return lbuf.at[oo, c, yy]

    def z_copy(d, zz, yy):
        oo = zz * 2 + x
        return rcopy(item(oo, yy), item(oo, yy), z_s.at[d, zz, yy], z_r.at[zz, yy], dev((z + 1 - 2 * d) * 2 + x, a))

    def x_copy(zz, yy):
        oo = zz * 2 + x
        return rcopy(item(oo, yy), item(oo, yy), x_s.at[zz, yy], x_r.at[zz, yy], x_peer)

    def x_wait(zz, yy):
        oo = zz * 2 + ox
        rcopy(item(oo, yy), item(oo, yy), x_s.at[zz, yy], x_r.at[zz, yy], x_peer).wait_recv()

    def s_copy(oo, yy):
        return rcopy(item(oo, yy), item(oo, yy), s_s.at[oo, yy], s_r.at[oo, yy], sibling)

    def s_wait(oo, yy):
        there = lbuf.at[oo, oc, yy]
        rcopy(there, there, s_s.at[oo, yy], s_r.at[oo, yy], sibling).wait_recv()

    def forward(zz, yy, right, left):
        @pl.when(jnp.logical_and(right, z + 1 < lines))
        def _():
            z_copy(0, zz, yy).start()

        @pl.when(jnp.logical_and(left, z > 0))
        def _():
            z_copy(1, zz, yy).start()

        x_copy(zz, yy).start()
        s_copy(zz * 2 + x, yy).start()

    def place(d, sign):
        zz = z - d + 2 * d * sign
        ok = jnp.logical_and(jnp.logical_and(zz >= 0, zz < lines), jnp.logical_or(d > 0, sign == 0))
        return zz, ok

    def stage(d, n):
        yy = (y + n) % 2
        for sign in range(2):
            zz, ok = place(d, sign)

            @pl.when(ok)
            def _():
                z_copy(0, zz, yy).wait_recv()
                forward(zz, yy, sign == 0, sign == 1)

    def across(d, n):
        yy = (y + n) % 2
        for sign in range(2):
            zz, ok = place(d, sign)

            @pl.when(ok)
            def _():
                x_wait(zz, yy)
                s_copy(zz * 2 + ox, yy).start()

    loads[0].wait()
    ky(oy).start()
    lbuf[o, c, y] = f_ref[y]
    forward(z, y, True, True)
    ky(y).start()
    kbuf[c, y] = f_ref[...]
    ksib(0, y, 0).start()
    ksib(1, y, 1).start()
    for load in loads[1:]:
        load.wait()

    slots = i_ref.shape[1]
    order = lax.broadcasted_iota(jnp.int32, (8, slots), 1)
    row_hit = jnp.logical_and(
        i_ref[...] == lax.broadcasted_iota(jnp.int32, (8, slots), 0), order < count_ref[0]
    )
    col_hit = partner_ref[...] * held + j_ref[...] == lax.broadcasted_iota(jnp.int32, (128, slots), 0)
    cnt_ref[...] = nt(row_hit.astype(f32).astype(bf16), col_hit.astype(f32).astype(bf16))
    cnt[o] = cnt_ref[...]

    def cnt_copy(oo):
        return rcopy(cnt_ref, cnt.at[o], cnt_s.at[oo], cnt_r.at[o], dev(oo, a))

    for s in range(1, occ_count):
        cnt_copy((o + s) % occ_count).start()

    ky_wait(y)
    lbuf[o, c, oy] = kbuf[c, oy, y]
    forward(z, oy, True, True)
    ksib(2, oy, y).start()
    stage(1, 0)
    across(0, 0)
    ky_wait(oy)
    ksib(3, oy, oy).start()
    stage(1, 1)
    across(0, 1)

    gacc[...] = jnp.zeros_like(gacc)
    for s in range(1, occ_count):
        oo = (o + s) % occ_count
        rcopy(cnt_ref, cnt.at[oo], cnt_s.at[oo], cnt_r.at[oo], dev(oo, a)).wait_recv()
    ksib_wait(0, y, 0)
    ksib_wait(1, y, 1)
    ksib_wait(2, oy, y)
    ksib_wait(3, oy, oy)
    for cc in range(2):
        for yy in range(2):
            for k in range(2):
                kh[cc, yy, k * half:(k + 1) * half] = kbuf[cc, yy, k, pl.ds(c * half, half)]
    vcol = jnp.broadcast_to(v_ref[:, pl.ds(pl.multiple_of(c * half, half), half)], (width, half)).T
    side[0:half] = vcol - e_ref[0, 2 * o]
    side[half:virtuals] = vcol - e_ref[0, 2 * o + 1]
    vrow = v_ref[...]
    rows8 = lax.broadcasted_iota(jnp.int32, cnt_ref.shape, 0)
    lanes8 = lax.broadcasted_iota(jnp.int32, cnt_ref.shape, 1)

    def pick(tile, row, lane):
        here = jnp.logical_and(rows8 == row, lanes8 == lane)
        return jnp.sum(jnp.where(here, tile, 0.0), keepdims=True)

    def work(oo):
        far = 2 * oo + y
        inter = nt(kh[0, 0], lbuf[oo, 0, 0])
        inter += nt(kh[0, 1], lbuf[oo, 0, 1])
        inter += nt(kh[1, 0], lbuf[oo, 1, 0])
        inter += nt(kh[1, 1], lbuf[oo, 1, 1])
        amplitude = (inter / (side[...] + (vrow - e_ref[0, far]))).astype(bf16)
        mine, theirs = cnt[o], cnt[oo]
        w1 = [pick(mine, k, far) for k in range(2)]
        w2 = [pick(theirs, y, 2 * o + k) for k in range(2)]
        for cc in range(2):
            for yy in range(2):
                term = jnp.dot(amplitude, lbuf[oo, cc, yy], preferred_element_type=f32)
                for k in range(2):
                    part = term[k * half:(k + 1) * half]
                    gacc[cc, yy, k * half:(k + 1) * half] += (
                        w1[k] * part + w2[k] * part.astype(bf16).astype(f32)
                    )

    def column(d, ox_side):
        def each(sign, carry):
            zz, ok = place(d, sign)
            oo = zz * 2 + (x + ox_side) % 2

            @pl.when(ok)
            def _():
                s_wait(oo, 0)
                s_wait(oo, 1)
                work(oo)

            return carry

        lax.fori_loop(0, 2, each, 0)

    column(0, 0)
    column(0, 1)

    def step(d, carry):
        def part(n, carry):
            @pl.when(d < lines)
            def _():
                stage(d, n)

            across(d - 1, n)
            column(d - 1, n)
            return carry

        return lax.fori_loop(0, 2, part, carry)

    lax.fori_loop(2, lines + 1, step, 0)

    out_width = aux_ref.shape[1]

    def cols(h):
        return slice(h * out_width, (h + 1) * out_width)

    def g_copy(h, cc):
        return rcopy(gsend.at[h, cc], grecv.at[h, cc], g_s.at[h, cc], g_r.at[h, cc], y_peer)

    def gs_copy(h):
        return rcopy(gfull.at[h], gsib.at[h], gs_s.at[h], gs_r.at[h], sibling)

    def a_copy(h, oo):
        return rcopy(asend.at[h, oo], arecv.at[h, o], a_s.at[h, oo], a_r.at[h, o], dev(oo, a))

    def t_copy(h):
        return rcopy(tsend.at[h], trecv.at[o % 2], t_s.at[h], t_r.at[o % 2], dev(2 * a + h, ta))

    def t_far(h):
        return jnp.logical_or(ta != a, o != 2 * a + h)

    for h in range(2):
        for n in range(2):
            cc = (c + 1 + n) % 2
            gsend[h, cc] = gacc[cc, oy][:, cols(h)].astype(bf16)
            g_copy(h, cc).start()

    for h in range(2):
        g_copy(h, oc).wait_recv()
        gfull[h] = gacc[oc, y][:, cols(h)] + grecv[h, oc].astype(f32)
        gs_copy(h).start()
        g_copy(h, c).wait_recv()
        mine = gacc[c, y][:, cols(h)] + grecv[h, c].astype(f32)
        for k in range(2):
            gamma_ref[k, pl.ds(c * half, half), cols(h)] = mine[k * half:(k + 1) * half]
        gs_copy(h).wait_recv()
        for k in range(2):
            gamma_ref[k, pl.ds(oc * half, half), cols(h)] = gsib[h, k * half:(k + 1) * half]
        rounded = gamma_ref[:, :, cols(h)].reshape(held * virtuals, out_width).astype(bf16)

        for n in range(4):
            block = (ta + 2 + n) % 4
            terms = tn(rounded, kbuf[block % 2, block // 2].reshape(held * virtuals, width))
            for g in range(2):
                oo = 2 * block + g
                part = terms[:, cols(g)]
                asend[h, oo] = part.astype(bf16)

                @pl.when(oo == o)
                def _():
                    aux_ref[cols(h)] = part

                @pl.when(oo != o)
                def _():
                    a_copy(h, oo).start()

    for h in range(2):
        total = aux_ref[cols(h)]
        for s in range(1, occ_count):
            oo = (o + s) % occ_count
            rcopy(asend.at[h, oo], arecv.at[h, oo], a_s.at[h, oo], a_r.at[h, oo], dev(oo, a)).wait_recv()
            total += arecv[h, oo].astype(f32)
        tsend[h] = total

        @pl.when(t_far(h))
        def _():
            t_copy(h).start()

        @pl.when(jnp.logical_not(t_far(h)))
        def _():
            trecv[o % 2] = tsend[h]

    scale = float(occ_count * held * virtuals) ** (-0.5)
    for h in range(2):
        @pl.when(t_far(h))
        def _():
            rcopy(tsend.at[h], trecv.at[h], t_s.at[h], t_r.at[h], dev(2 * a + h, ta)).wait_recv()

        aux_ref[cols(h)] = (tsend[h] + trecv[h].T) * scale

    for r in range(2):
        ky(r).wait_send()
        g_copy(r, 0).wait_send()
        g_copy(r, 1).wait_send()
        gs_copy(r).wait_send()
    ksib(0, y, 0).wait_send()
    ksib(1, y, 1).wait_send()
    ksib(2, oy, y).wait_send()
    ksib(3, oy, oy).wait_send()
    for s in range(1, occ_count):
        oo = (o + s) % occ_count
        cnt_copy(oo).wait_send()
        a_copy(0, oo).wait_send()
        a_copy(1, oo).wait_send()
    for h in range(2):
        @pl.when(t_far(h))
        def _():
            t_copy(h).wait_send()

    def drain(zz, carry):
        for yy in range(2):
            @pl.when(jnp.logical_and(zz <= z, z + 1 < lines))
            def _():
                z_copy(0, zz, yy).wait_send()

            @pl.when(jnp.logical_and(zz >= z, z > 0))
            def _():
                z_copy(1, zz, yy).wait_send()

            x_copy(zz, yy).wait_send()
            s_copy(zz * 2, yy).wait_send()
            s_copy(zz * 2 + 1, yy).wait_send()
        return carry

    lax.fori_loop(0, lines, drain, 0)


def table_body(factors, occ_energy, vir_energy, i_slot, j_slot, partner_device, pair_count):
    held, virtuals, width = factors.shape
    slots = i_slot.shape[0]
    orbitals = occ_energy.shape[0]
    occ_count = lax.axis_size("occ")
    lines = occ_count // 2
    out_width = 4 * width // occ_count
    vmem = pl.BlockSpec(memory_space=pltpu.VMEM)
    dma = pltpu.SemaphoreType.DMA
    return pl.pallas_call(
        kernel,
        out_shape=(
            jax.ShapeDtypeStruct((held, virtuals, width), f32),
            jax.ShapeDtypeStruct((width, out_width), f32),
        ),
        in_specs=[pl.BlockSpec(memory_space=pltpu.HBM)] * 6 + [pl.BlockSpec(memory_space=pltpu.SMEM)],
        out_specs=(vmem, vmem),
        scratch_shapes=[
            pltpu.VMEM((2, 2, held, virtuals, width), bf16),
            pltpu.VMEM((occ_count, 2, 2, virtuals, width), bf16),
            pltpu.VMEM((2, 2, virtuals, width), bf16),
            pltpu.VMEM((occ_count, 8, 128), f32),
            pltpu.VMEM((2, 2, virtuals, width), f32),
            pltpu.VMEM((2, 2, virtuals, out_width), bf16),
            pltpu.VMEM((2, 2, virtuals, out_width), bf16),
            pltpu.VMEM((2, virtuals, out_width), f32),
            pltpu.VMEM((2, virtuals, out_width), f32),
            pltpu.VMEM((2, occ_count, out_width, out_width), bf16),
            pltpu.VMEM((2, occ_count, out_width, out_width), bf16),
            pltpu.VMEM((2, out_width, out_width), f32),
            pltpu.VMEM((2, out_width, out_width), f32),
            dma((2,)), dma((2,)), dma((4,)), dma((4,)),
            dma((2, lines, 2)), dma((lines, 2)), dma((lines, 2)), dma((lines, 2)),
            dma((occ_count, 2)), dma((occ_count, 2)),
            dma((occ_count,)), dma((occ_count,)), dma((2, 2)), dma((2, 2)), dma((2,)), dma((2,)),
            dma((2, occ_count)), dma((2, occ_count)), dma((2,)), dma((2,)),
            pltpu.VMEM((held, virtuals, width), bf16),
            pltpu.SMEM((1, orbitals), f32),
            pltpu.VMEM((1, virtuals), f32),
            pltpu.VMEM((1, slots), jnp.int32),
            pltpu.VMEM((1, slots), jnp.int32),
            pltpu.VMEM((1, slots), jnp.int32),
            pltpu.VMEM((8, 128), f32),
            pltpu.VMEM((virtuals, virtuals), f32),
            dma((6,)),
        ],
        compiler_params=pltpu.CompilerParams(
            collective_id=0, has_side_effects=True, vmem_limit_bytes=64 * 1024 * 1024
        ),
    )(
        factors, occ_energy[None, :], vir_energy[None, :], i_slot[None, :], j_slot[None, :],
        partner_device.reshape(1, slots), pair_count,
    )


def body(*operands):
    factors, i_slot = operands[0], operands[3]
    held, virtuals, width = factors.shape
    occ_count, aux_count = lax.axis_size("occ"), lax.axis_size("aux")
    orbitals = held * occ_count
    fits = (
        held == 2 and aux_count == 4 and occ_count == 2 * aux_count and orbitals <= 128
        and orbitals * orbitals <= occ_count * i_slot.shape[0]
        and virtuals == width and width % 256 == 0 and 4 * width == occ_count * 128
    )
    return table_body(*operands) if fits else slot_body(*operands)


def solution(mesh):
    placed = (P("occ", None, "aux"), P(), P(), P("occ"), P("occ"), P("occ", None), P("occ"))
    return jax.shard_map(
        body,
        mesh=mesh,
        in_specs=placed,
        out_specs=(P("occ", None, "aux"), P("aux", "occ")),
        check_vma=False,
    )
```

```python
import jax
import jax.numpy as jnp
from jax import lax
from jax.experimental import pallas as pl
from jax.experimental.pallas import tpu as pltpu
from jax.sharding import PartitionSpec as P

MESH = pl.DeviceIdType.MESH
f32 = jnp.float32
bf16 = jnp.bfloat16


def slot_body(factors, occ_energy, vir_energy, i_slot, j_slot, partner_device, pair_count):
    held, virtuals, columns = factors.shape
    pair_slots = i_slot.shape[0]
    occ_count = lax.axis_size("occ")
    capacity = max(2, (3 * pair_slots // 2 + occ_count - 1) // occ_count)
    slot_total = occ_count * capacity
    device_index = lax.axis_index("occ")
    pair_order = jnp.arange(pair_slots, dtype=jnp.int32)
    living = pair_order < pair_count[0]
    target = partner_device[:, 0]
    earlier = (
        (target[:, None] == target[None, :])
        & living[None, :]
        & (pair_order[None, :] < pair_order[:, None])
    )
    slot_rank = jnp.sum(earlier.astype(jnp.int32), axis=1)
    slot_index = target * capacity + slot_rank
    slot_hit = (slot_index[:, None] == jnp.arange(slot_total, dtype=jnp.int32)[None, :]) & living[
        :, None
    ]
    requests = jnp.sum(jnp.where(slot_hit, j_slot[:, None] + 1, 0), axis=0) - 1
    wanted = lax.all_to_all(requests, "occ", split_axis=0, concat_axis=0, tiled=True)
    wanted_hit = (wanted[:, None] == jnp.arange(held, dtype=jnp.int32)[None, :]).astype(
        jnp.bfloat16
    )
    far_index = target * held + j_slot
    piece = lax.all_gather(factors, "occ", axis=0, tiled=True)
    count = piece.shape[0]
    hit = (far_index[:, None] == jnp.arange(count, dtype=jnp.int32)[None, :]).astype(jnp.bfloat16)
    gathered = jnp.dot(
        hit, piece.reshape(count, virtuals * columns), preferred_element_type=jnp.float32
    )
    partner_blocks = gathered.astype(jnp.bfloat16).reshape(pair_slots, virtuals, columns)
    own_blocks = factors[i_slot]
    orbitals = occ_energy.shape[0]
    table = jnp.arange(orbitals, dtype=jnp.int32)
    own_index = device_index * held + i_slot
    energy_own = jnp.sum(
        jnp.where(own_index[:, None] == table[None, :], occ_energy[None, :], 0.0), axis=1
    )
    energy_far = jnp.sum(
        jnp.where(far_index[:, None] == table[None, :], occ_energy[None, :], 0.0), axis=1
    )
    denominator = (
        vir_energy[None, :, None]
        + vir_energy[None, None, :]
        - energy_own[:, None, None]
        - energy_far[:, None, None]
    )
    partial_value = jnp.einsum(
        "pvq,pwq->pvw", own_blocks, partner_blocks, preferred_element_type=jnp.float32
    )
    summed = lax.psum(partial_value, "aux")
    amplitude = jnp.where(living[:, None, None], summed / denominator, 0.0).astype(jnp.bfloat16)
    local_terms = jnp.einsum(
        "pvw,pwq->pvq", amplitude, partner_blocks, preferred_element_type=jnp.float32
    )
    owner_hit = (i_slot[:, None] == jnp.arange(held, dtype=jnp.int32)[None, :]).astype(jnp.float32)
    gamma_local = jnp.einsum("po,pvq->ovq", owner_hit, local_terms, precision=lax.Precision.HIGHEST)
    return_terms = jnp.einsum(
        "pwv,pwq->pvq", amplitude, own_blocks, preferred_element_type=jnp.float32
    ).astype(jnp.bfloat16)
    placed = jnp.dot(
        slot_hit.astype(jnp.bfloat16).T,
        return_terms.reshape(pair_slots, virtuals * columns),
        preferred_element_type=jnp.float32,
    )
    placed = placed.astype(jnp.bfloat16).reshape(slot_total, virtuals, columns)
    returned = lax.all_to_all(placed, "occ", split_axis=0, concat_axis=0, tiled=True)
    gathered_back = jnp.dot(
        wanted_hit.T,
        returned.reshape(slot_total, virtuals * columns),
        preferred_element_type=jnp.float32,
    )
    gamma = gamma_local + gathered_back.reshape(held, virtuals, columns)
    rounded = gamma.astype(jnp.bfloat16)
    stacked = jnp.stack([rounded, factors])
    gamma_rows = rounded.reshape(held * virtuals, columns)
    factor_flat = factors.reshape(held * virtuals, columns)
    piece = lax.all_gather(stacked, "aux", axis=3, tiled=True)
    width_here = piece.shape[3]
    gamma_piece = piece[0].reshape(held * virtuals, width_here)
    factor_piece = piece[1].reshape(held * virtuals, width_here)
    first = jnp.dot(gamma_rows.T, factor_piece, preferred_element_type=jnp.float32)
    second = jnp.dot(factor_flat.T, gamma_piece, preferred_element_type=jnp.float32)
    terms = first + second
    shared = lax.psum_scatter(terms, "occ", scatter_dimension=1, tiled=True)
    factor_scale = float(orbitals * virtuals) ** (-0.5)
    return (gamma, shared * factor_scale)


def nt(a, b):
    return lax.dot_general(a, b, (((1,), (1,)), ((), ())), preferred_element_type=f32)


def tn(a, b):
    return lax.dot_general(a, b, (((0,), (0,)), ((), ())), preferred_element_type=f32)


def kernel(
    f_hbm, e_hbm, v_hbm, i_hbm, j_hbm, partner_hbm, count_ref,
    gamma_ref, aux_ref,
    kbuf, lbuf, kh, cnt, gacc, gsend, grecv, gfull, gsib, axsend, axrecv, akeep, azsend, azrecv, tsend, trecv,
    ky_s, ky_r, ksib_s, ksib_r, z_s, z_r, x_s, x_r, s_s, s_r,
    cnt_s, cnt_r, g_s, g_r, gs_s, gs_r, ax_s, ax_r, az_s, az_r, t_s, t_r,
    f_ref, e_ref, v_ref, i_ref, j_ref, partner_ref, cnt_ref, side, in_s,
):
    occ_count = lax.axis_size("occ")
    lines = occ_count // 2
    held, virtuals, width = f_ref.shape
    half = virtuals // 2
    o = lax.axis_index("occ")
    a = lax.axis_index("aux")
    z, x = o // 2, o % 2
    y, c = a // 2, a % 2
    oy, oc, ox = 1 - y, 1 - c, 1 - x

    def dev(occ, aux):
        return {"occ": occ, "aux": aux}

    y_peer, sibling = dev(o, oy * 2 + c), dev(o, y * 2 + oc)
    x_peer = dev(z * 2 + ox, a)

    def rcopy(src, dst, ss, rs, target):
        return pltpu.make_async_remote_copy(
            src_ref=src, dst_ref=dst, send_sem=ss, recv_sem=rs, device_id=target, device_id_type=MESH
        )

    pairs = (
        (f_hbm, f_ref), (e_hbm, e_ref), (v_hbm, v_ref), (i_hbm, i_ref), (j_hbm, j_ref),
        (partner_hbm, partner_ref),
    )
    loads = [pltpu.make_async_copy(there, here, in_s.at[n]) for n, (there, here) in enumerate(pairs)]
    for load in loads:
        load.start()

    barrier = pltpu.get_barrier_semaphore()
    for s in range(1, occ_count):
        pl.semaphore_signal(barrier, inc=1, device_id=dev((o + s) % occ_count, a), device_id_type=MESH)
    pl.semaphore_signal(barrier, inc=1, device_id=y_peer, device_id_type=MESH)
    pl.semaphore_signal(barrier, inc=1, device_id=sibling, device_id_type=MESH)
    ta = o // 2
    for h in range(2):
        @pl.when(jnp.logical_or(ta != a, o != 2 * a + h))
        def _():
            pl.semaphore_signal(barrier, inc=1, device_id=dev(2 * a + h, ta), device_id_type=MESH)
    pl.semaphore_wait(barrier, occ_count + 1 + jnp.where(ta != a, 2, 1))

    def ky(r):
        return rcopy(f_ref.at[r], kbuf.at[c, y, r], ky_s.at[r], ky_r.at[r], y_peer)

    def ky_wait(r):
        rcopy(f_ref.at[r], kbuf.at[c, oy, r], ky_s.at[r], ky_r.at[r], y_peer).wait_recv()

    def ksib(n, yy, r):
        return rcopy(kbuf.at[c, yy, r], kbuf.at[c, yy, r], ksib_s.at[n], ksib_r.at[n], sibling)

    def ksib_wait(n, yy, r):
        rcopy(kbuf.at[oc, yy, r], kbuf.at[oc, yy, r], ksib_s.at[n], ksib_r.at[n], sibling).wait_recv()

    def item(oo, yy):
        return lbuf.at[oo, c, yy]

    def z_copy(d, zz, yy):
        oo = zz * 2 + x
        return rcopy(item(oo, yy), item(oo, yy), z_s.at[d, zz, yy], z_r.at[zz, yy], dev((z + 1 - 2 * d) * 2 + x, a))

    def x_copy(zz, yy):
        oo = zz * 2 + x
        return rcopy(item(oo, yy), item(oo, yy), x_s.at[zz, yy], x_r.at[zz, yy], x_peer)

    def x_wait(zz, yy):
        oo = zz * 2 + ox
        rcopy(item(oo, yy), item(oo, yy), x_s.at[zz, yy], x_r.at[zz, yy], x_peer).wait_recv()

    def s_copy(oo, yy):
        return rcopy(item(oo, yy), item(oo, yy), s_s.at[oo, yy], s_r.at[oo, yy], sibling)

    def s_wait(oo, yy):
        there = lbuf.at[oo, oc, yy]
        rcopy(there, there, s_s.at[oo, yy], s_r.at[oo, yy], sibling).wait_recv()

    def forward(zz, yy, right, left):
        @pl.when(jnp.logical_and(right, z + 1 < lines))
        def _():
            z_copy(0, zz, yy).start()

        @pl.when(jnp.logical_and(left, z > 0))
        def _():
            z_copy(1, zz, yy).start()

        x_copy(zz, yy).start()
        s_copy(zz * 2 + x, yy).start()

    def place(d, sign):
        zz = z - d + 2 * d * sign
        ok = jnp.logical_and(jnp.logical_and(zz >= 0, zz < lines), jnp.logical_or(d > 0, sign == 0))
        return zz, ok

    def stage(d, n):
        yy = (y + n) % 2
        for sign in range(2):
            zz, ok = place(d, sign)

            @pl.when(ok)
            def _():
                z_copy(0, zz, yy).wait_recv()
                forward(zz, yy, sign == 0, sign == 1)

    def across(d, n):
        yy = (y + n) % 2
        for sign in range(2):
            zz, ok = place(d, sign)

            @pl.when(ok)
            def _():
                x_wait(zz, yy)
                s_copy(zz * 2 + ox, yy).start()

    loads[0].wait()
    ky(oy).start()
    lbuf[o, c, y] = f_ref[y]
    forward(z, y, True, True)
    ky(y).start()
    kbuf[c, y] = f_ref[...]
    ksib(0, y, 0).start()
    ksib(1, y, 1).start()
    for load in loads[1:]:
        load.wait()

    slots = i_ref.shape[1]
    order = lax.broadcasted_iota(jnp.int32, (8, slots), 1)
    row_hit = jnp.logical_and(
        i_ref[...] == lax.broadcasted_iota(jnp.int32, (8, slots), 0), order < count_ref[0]
    )
    col_hit = partner_ref[...] * held + j_ref[...] == lax.broadcasted_iota(jnp.int32, (128, slots), 0)
    cnt_ref[...] = nt(row_hit.astype(f32).astype(bf16), col_hit.astype(f32).astype(bf16))
    cnt[o] = cnt_ref[...]

    def cnt_copy(oo):
        return rcopy(cnt_ref, cnt.at[o], cnt_s.at[oo], cnt_r.at[o], dev(oo, a))

    for s in range(1, occ_count):
        cnt_copy((o + s) % occ_count).start()

    ky_wait(y)
    lbuf[o, c, oy] = kbuf[c, oy, y]
    forward(z, oy, True, True)
    ksib(2, oy, y).start()
    stage(1, 0)
    across(0, 0)
    ky_wait(oy)
    ksib(3, oy, oy).start()
    stage(1, 1)
    across(0, 1)

    gacc[...] = jnp.zeros_like(gacc)
    for s in range(1, occ_count):
        oo = (o + s) % occ_count
        rcopy(cnt_ref, cnt.at[oo], cnt_s.at[oo], cnt_r.at[oo], dev(oo, a)).wait_recv()
    ksib_wait(0, y, 0)
    ksib_wait(1, y, 1)
    ksib_wait(2, oy, y)
    ksib_wait(3, oy, oy)
    for cc in range(2):
        for yy in range(2):
            for k in range(2):
                kh[cc, yy, k * half:(k + 1) * half] = kbuf[cc, yy, k, pl.ds(c * half, half)]
    vcol = jnp.broadcast_to(v_ref[:, pl.ds(pl.multiple_of(c * half, half), half)], (width, half)).T
    side[0:half] = vcol - e_ref[0, 2 * o]
    side[half:virtuals] = vcol - e_ref[0, 2 * o + 1]
    vrow = v_ref[...]
    rows8 = lax.broadcasted_iota(jnp.int32, cnt_ref.shape, 0)
    lanes8 = lax.broadcasted_iota(jnp.int32, cnt_ref.shape, 1)

    def pick(tile, row, lane):
        here = jnp.logical_and(rows8 == row, lanes8 == lane)
        return jnp.sum(jnp.where(here, tile, 0.0), keepdims=True)

    def work(oo):
        far = 2 * oo + y
        inter = nt(kh[0, 0], lbuf[oo, 0, 0])
        inter += nt(kh[0, 1], lbuf[oo, 0, 1])
        inter += nt(kh[1, 0], lbuf[oo, 1, 0])
        inter += nt(kh[1, 1], lbuf[oo, 1, 1])
        amplitude = (inter / (side[...] + (vrow - e_ref[0, far]))).astype(bf16)
        mine, theirs = cnt[o], cnt[oo]
        w1 = [pick(mine, k, far) for k in range(2)]
        w2 = [pick(theirs, y, 2 * o + k) for k in range(2)]
        for cc in range(2):
            for yy in range(2):
                term = jnp.dot(amplitude, lbuf[oo, cc, yy], preferred_element_type=f32)
                for k in range(2):
                    part = term[k * half:(k + 1) * half]
                    gacc[cc, yy, k * half:(k + 1) * half] += (
                        w1[k] * part + w2[k] * part.astype(bf16).astype(f32)
                    )

    def column(d, ox_side):
        def each(sign, carry):
            zz, ok = place(d, sign)
            oo = zz * 2 + (x + ox_side) % 2

            @pl.when(ok)
            def _():
                s_wait(oo, 0)
                s_wait(oo, 1)
                work(oo)

            return carry

        lax.fori_loop(0, 2, each, 0)

    column(0, 0)
    column(0, 1)

    def step(d, carry):
        def part(n, carry):
            @pl.when(d < lines)
            def _():
                stage(d, n)

            across(d - 1, n)
            column(d - 1, n)
            return carry

        return lax.fori_loop(0, 2, part, carry)

    lax.fori_loop(2, lines + 1, step, 0)

    out_width = aux_ref.shape[1]

    def cols(h):
        return slice(h * out_width, (h + 1) * out_width)

    def g_copy(h, cc):
        return rcopy(gsend.at[h, cc], grecv.at[h, cc], g_s.at[h, cc], g_r.at[h, cc], y_peer)

    def gs_copy(h):
        return rcopy(gfull.at[h], gsib.at[h], gs_s.at[h], gs_r.at[h], sibling)

    def ax_copy(h, b):
        return rcopy(axsend.at[h, b], axrecv.at[h, b], ax_s.at[h, b], ax_r.at[h, b], x_peer)

    def az_copy(h, b):
        return rcopy(azsend.at[h, b], azrecv.at[h, z], az_s.at[h, b], az_r.at[h, z], dev(b * 2 + x, a))

    def t_copy(h):
        return rcopy(tsend.at[h], trecv.at[o % 2], t_s.at[h], t_r.at[o % 2], dev(2 * a + h, ta))

    def t_far(h):
        return jnp.logical_or(ta != a, o != 2 * a + h)

    for h in range(2):
        for n in range(2):
            cc = (c + 1 + n) % 2
            gsend[h, cc] = gacc[cc, oy][:, cols(h)].astype(bf16)
            g_copy(h, cc).start()

    for h in range(2):
        g_copy(h, oc).wait_recv()
        gfull[h] = gacc[oc, y][:, cols(h)] + grecv[h, oc].astype(f32)
        gs_copy(h).start()
        g_copy(h, c).wait_recv()
        mine = gacc[c, y][:, cols(h)] + grecv[h, c].astype(f32)
        for k in range(2):
            gamma_ref[k, pl.ds(c * half, half), cols(h)] = mine[k * half:(k + 1) * half]
        gs_copy(h).wait_recv()
        for k in range(2):
            gamma_ref[k, pl.ds(oc * half, half), cols(h)] = gsib[h, k * half:(k + 1) * half]
        rounded = gamma_ref[:, :, cols(h)].reshape(held * virtuals, out_width).astype(bf16)

        for n in range(4):
            block = (ta + 2 + n) % 4
            terms = tn(rounded, kbuf[block % 2, block // 2].reshape(held * virtuals, width))
            low, high = terms[:, cols(0)], terms[:, cols(1)]
            axsend[h, block] = jnp.where(x == 0, high, low).astype(bf16)
            ax_copy(h, block).start()
            akeep[h, block] = jnp.where(x == 0, low, high)

    for h in range(2):
        for n in range(4):
            block = (ta + 2 + n) % 4
            ax_copy(h, block).wait_recv()
            pair = akeep[h, block] + axrecv[h, block].astype(f32)
            if n == 2:
                akeep[h, block] = pair
            else:
                azsend[h, block] = pair.astype(bf16)
                az_copy(h, block).start()

    for h in range(2):
        total = akeep[h, z]
        for n in range(1, lines):
            zz = (z + n) % lines
            rcopy(azsend.at[h, zz], azrecv.at[h, zz], az_s.at[h, zz], az_r.at[h, zz], dev(zz * 2 + x, a)).wait_recv()
            total += azrecv[h, zz].astype(f32)
        tsend[h] = total

        @pl.when(t_far(h))
        def _():
            t_copy(h).start()

        @pl.when(jnp.logical_not(t_far(h)))
        def _():
            trecv[o % 2] = tsend[h]

    scale = float(occ_count * held * virtuals) ** (-0.5)
    for h in range(2):
        @pl.when(t_far(h))
        def _():
            rcopy(tsend.at[h], trecv.at[h], t_s.at[h], t_r.at[h], dev(2 * a + h, ta)).wait_recv()

        aux_ref[cols(h)] = (tsend[h] + trecv[h].T) * scale

    for r in range(2):
        ky(r).wait_send()
        g_copy(r, 0).wait_send()
        g_copy(r, 1).wait_send()
        gs_copy(r).wait_send()
    ksib(0, y, 0).wait_send()
    ksib(1, y, 1).wait_send()
    ksib(2, oy, y).wait_send()
    ksib(3, oy, oy).wait_send()
    for s in range(1, occ_count):
        oo = (o + s) % occ_count
        cnt_copy(oo).wait_send()
    for h in range(2):
        @pl.when(t_far(h))
        def _():
            t_copy(h).wait_send()

        for n in range(lines):
            block = (z + n) % lines
            ax_copy(h, block).wait_send()
            if n > 0:
                az_copy(h, block).wait_send()

    def drain(zz, carry):
        for yy in range(2):
            @pl.when(jnp.logical_and(zz <= z, z + 1 < lines))
            def _():
                z_copy(0, zz, yy).wait_send()

            @pl.when(jnp.logical_and(zz >= z, z > 0))
            def _():
                z_copy(1, zz, yy).wait_send()

            x_copy(zz, yy).wait_send()
            s_copy(zz * 2, yy).wait_send()
            s_copy(zz * 2 + 1, yy).wait_send()
        return carry

    lax.fori_loop(0, lines, drain, 0)


def table_body(factors, occ_energy, vir_energy, i_slot, j_slot, partner_device, pair_count):
    held, virtuals, width = factors.shape
    slots = i_slot.shape[0]
    orbitals = occ_energy.shape[0]
    occ_count = lax.axis_size("occ")
    lines = occ_count // 2
    out_width = 4 * width // occ_count
    vmem = pl.BlockSpec(memory_space=pltpu.VMEM)
    dma = pltpu.SemaphoreType.DMA
    return pl.pallas_call(
        kernel,
        out_shape=(
            jax.ShapeDtypeStruct((held, virtuals, width), f32),
            jax.ShapeDtypeStruct((width, out_width), f32),
        ),
        in_specs=[pl.BlockSpec(memory_space=pltpu.HBM)] * 6 + [pl.BlockSpec(memory_space=pltpu.SMEM)],
        out_specs=(vmem, vmem),
        scratch_shapes=[
            pltpu.VMEM((2, 2, held, virtuals, width), bf16),
            pltpu.VMEM((occ_count, 2, 2, virtuals, width), bf16),
            pltpu.VMEM((2, 2, virtuals, width), bf16),
            pltpu.VMEM((occ_count, 8, 128), f32),
            pltpu.VMEM((2, 2, virtuals, width), f32),
            pltpu.VMEM((2, 2, virtuals, out_width), bf16),
            pltpu.VMEM((2, 2, virtuals, out_width), bf16),
            pltpu.VMEM((2, virtuals, out_width), f32),
            pltpu.VMEM((2, virtuals, out_width), f32),
            pltpu.VMEM((2, lines, out_width, out_width), bf16),
            pltpu.VMEM((2, lines, out_width, out_width), bf16),
            pltpu.VMEM((2, lines, out_width, out_width), f32),
            pltpu.VMEM((2, lines, out_width, out_width), bf16),
            pltpu.VMEM((2, lines, out_width, out_width), bf16),
            pltpu.VMEM((2, out_width, out_width), f32),
            pltpu.VMEM((2, out_width, out_width), f32),
            dma((2,)), dma((2,)), dma((4,)), dma((4,)),
            dma((2, lines, 2)), dma((lines, 2)), dma((lines, 2)), dma((lines, 2)),
            dma((occ_count, 2)), dma((occ_count, 2)),
            dma((occ_count,)), dma((occ_count,)), dma((2, 2)), dma((2, 2)), dma((2,)), dma((2,)),
            dma((2, lines)), dma((2, lines)), dma((2, lines)), dma((2, lines)), dma((2,)), dma((2,)),
            pltpu.VMEM((held, virtuals, width), bf16),
            pltpu.SMEM((1, orbitals), f32),
            pltpu.VMEM((1, virtuals), f32),
            pltpu.VMEM((1, slots), jnp.int32),
            pltpu.VMEM((1, slots), jnp.int32),
            pltpu.VMEM((1, slots), jnp.int32),
            pltpu.VMEM((8, 128), f32),
            pltpu.VMEM((virtuals, virtuals), f32),
            dma((6,)),
        ],
        compiler_params=pltpu.CompilerParams(
            collective_id=0, has_side_effects=True, vmem_limit_bytes=64 * 1024 * 1024
        ),
    )(
        factors, occ_energy[None, :], vir_energy[None, :], i_slot[None, :], j_slot[None, :],
        partner_device.reshape(1, slots), pair_count,
    )


def body(*operands):
    factors, i_slot = operands[0], operands[3]
    held, virtuals, width = factors.shape
    occ_count, aux_count = lax.axis_size("occ"), lax.axis_size("aux")
    orbitals = held * occ_count
    fits = (
        held == 2 and aux_count == 4 and occ_count == 2 * aux_count and orbitals <= 128
        and orbitals * orbitals <= occ_count * i_slot.shape[0]
        and virtuals == width and width % 256 == 0 and 4 * width == occ_count * 128
    )
    return table_body(*operands) if fits else slot_body(*operands)


def solution(mesh):
    placed = (P("occ", None, "aux"), P(), P(), P("occ"), P("occ"), P("occ", None), P("occ"))
    return jax.shard_map(
        body,
        mesh=mesh,
        in_specs=placed,
        out_specs=(P("occ", None, "aux"), P("aux", "occ")),
        check_vma=False,
    )
```

```python
import jax
import jax.numpy as jnp
from jax import lax
from jax.experimental import pallas as pl
from jax.experimental.pallas import tpu as pltpu
from jax.sharding import PartitionSpec as P

MESH = pl.DeviceIdType.MESH
f32 = jnp.float32
bf16 = jnp.bfloat16


def slot_body(factors, occ_energy, vir_energy, i_slot, j_slot, partner_device, pair_count):
    held, virtuals, columns = factors.shape
    pair_slots = i_slot.shape[0]
    occ_count = lax.axis_size("occ")
    capacity = max(2, (3 * pair_slots // 2 + occ_count - 1) // occ_count)
    slot_total = occ_count * capacity
    device_index = lax.axis_index("occ")
    pair_order = jnp.arange(pair_slots, dtype=jnp.int32)
    living = pair_order < pair_count[0]
    target = partner_device[:, 0]
    earlier = (
        (target[:, None] == target[None, :])
        & living[None, :]
        & (pair_order[None, :] < pair_order[:, None])
    )
    slot_rank = jnp.sum(earlier.astype(jnp.int32), axis=1)
    slot_index = target * capacity + slot_rank
    slot_hit = (slot_index[:, None] == jnp.arange(slot_total, dtype=jnp.int32)[None, :]) & living[
        :, None
    ]
    requests = jnp.sum(jnp.where(slot_hit, j_slot[:, None] + 1, 0), axis=0) - 1
    wanted = lax.all_to_all(requests, "occ", split_axis=0, concat_axis=0, tiled=True)
    wanted_hit = (wanted[:, None] == jnp.arange(held, dtype=jnp.int32)[None, :]).astype(
        jnp.bfloat16
    )
    far_index = target * held + j_slot
    piece = lax.all_gather(factors, "occ", axis=0, tiled=True)
    count = piece.shape[0]
    hit = (far_index[:, None] == jnp.arange(count, dtype=jnp.int32)[None, :]).astype(jnp.bfloat16)
    gathered = jnp.dot(
        hit, piece.reshape(count, virtuals * columns), preferred_element_type=jnp.float32
    )
    partner_blocks = gathered.astype(jnp.bfloat16).reshape(pair_slots, virtuals, columns)
    own_blocks = factors[i_slot]
    orbitals = occ_energy.shape[0]
    table = jnp.arange(orbitals, dtype=jnp.int32)
    own_index = device_index * held + i_slot
    energy_own = jnp.sum(
        jnp.where(own_index[:, None] == table[None, :], occ_energy[None, :], 0.0), axis=1
    )
    energy_far = jnp.sum(
        jnp.where(far_index[:, None] == table[None, :], occ_energy[None, :], 0.0), axis=1
    )
    denominator = (
        vir_energy[None, :, None]
        + vir_energy[None, None, :]
        - energy_own[:, None, None]
        - energy_far[:, None, None]
    )
    partial_value = jnp.einsum(
        "pvq,pwq->pvw", own_blocks, partner_blocks, preferred_element_type=jnp.float32
    )
    summed = lax.psum(partial_value, "aux")
    amplitude = jnp.where(living[:, None, None], summed / denominator, 0.0).astype(jnp.bfloat16)
    local_terms = jnp.einsum(
        "pvw,pwq->pvq", amplitude, partner_blocks, preferred_element_type=jnp.float32
    )
    owner_hit = (i_slot[:, None] == jnp.arange(held, dtype=jnp.int32)[None, :]).astype(jnp.float32)
    gamma_local = jnp.einsum("po,pvq->ovq", owner_hit, local_terms, precision=lax.Precision.HIGHEST)
    return_terms = jnp.einsum(
        "pwv,pwq->pvq", amplitude, own_blocks, preferred_element_type=jnp.float32
    ).astype(jnp.bfloat16)
    placed = jnp.dot(
        slot_hit.astype(jnp.bfloat16).T,
        return_terms.reshape(pair_slots, virtuals * columns),
        preferred_element_type=jnp.float32,
    )
    placed = placed.astype(jnp.bfloat16).reshape(slot_total, virtuals, columns)
    returned = lax.all_to_all(placed, "occ", split_axis=0, concat_axis=0, tiled=True)
    gathered_back = jnp.dot(
        wanted_hit.T,
        returned.reshape(slot_total, virtuals * columns),
        preferred_element_type=jnp.float32,
    )
    gamma = gamma_local + gathered_back.reshape(held, virtuals, columns)
    rounded = gamma.astype(jnp.bfloat16)
    stacked = jnp.stack([rounded, factors])
    gamma_rows = rounded.reshape(held * virtuals, columns)
    factor_flat = factors.reshape(held * virtuals, columns)
    piece = lax.all_gather(stacked, "aux", axis=3, tiled=True)
    width_here = piece.shape[3]
    gamma_piece = piece[0].reshape(held * virtuals, width_here)
    factor_piece = piece[1].reshape(held * virtuals, width_here)
    first = jnp.dot(gamma_rows.T, factor_piece, preferred_element_type=jnp.float32)
    second = jnp.dot(factor_flat.T, gamma_piece, preferred_element_type=jnp.float32)
    terms = first + second
    shared = lax.psum_scatter(terms, "occ", scatter_dimension=1, tiled=True)
    factor_scale = float(orbitals * virtuals) ** (-0.5)
    return (gamma, shared * factor_scale)


def nt(a, b):
    return lax.dot_general(a, b, (((1,), (1,)), ((), ())), preferred_element_type=f32)


def tn(a, b):
    return lax.dot_general(a, b, (((0,), (0,)), ((), ())), preferred_element_type=f32)


def kernel(
    f_hbm, e_hbm, v_hbm, i_hbm, j_hbm, partner_hbm, count_ref,
    gamma_ref, aux_ref,
    kbuf, lbuf, kh, cnt, gacc, gsend, grecv, gfull, gsib, axsend, axrecv, akeep, azsend, azrecv, near, nearin, tsend, trecv,
    ky_s, ky_r, ksib_s, ksib_r, z_s, z_r, x_s, x_r, s_s, s_r,
    cnt_s, cnt_r, g_s, g_r, gs_s, gs_r, ax_s, ax_r, az_s, az_r, t_s, t_r, w_s, w_r, n_s, n_r,
    f_ref, e_ref, v_ref, i_ref, j_ref, partner_ref, cnt_ref, side, in_s,
):
    occ_count = lax.axis_size("occ")
    lines = occ_count // 2
    held, virtuals, width = f_ref.shape
    half = virtuals // 2
    o = lax.axis_index("occ")
    a = lax.axis_index("aux")
    z, x = o // 2, o % 2
    y, c = a // 2, a % 2
    oy, oc, ox = 1 - y, 1 - c, 1 - x

    def dev(occ, aux):
        return {"occ": occ, "aux": aux}

    y_peer, sibling = dev(o, oy * 2 + c), dev(o, y * 2 + oc)
    x_peer = dev(z * 2 + ox, a)

    def rcopy(src, dst, ss, rs, target):
        return pltpu.make_async_remote_copy(
            src_ref=src, dst_ref=dst, send_sem=ss, recv_sem=rs, device_id=target, device_id_type=MESH
        )

    pairs = (
        (f_hbm, f_ref), (e_hbm, e_ref), (v_hbm, v_ref), (i_hbm, i_ref), (j_hbm, j_ref),
        (partner_hbm, partner_ref),
    )
    loads = [pltpu.make_async_copy(there, here, in_s.at[n]) for n, (there, here) in enumerate(pairs)]
    for load in loads:
        load.start()

    barrier = pltpu.get_barrier_semaphore()
    for s in range(1, occ_count):
        pl.semaphore_signal(barrier, inc=1, device_id=dev((o + s) % occ_count, a), device_id_type=MESH)
    pl.semaphore_signal(barrier, inc=1, device_id=y_peer, device_id_type=MESH)
    pl.semaphore_signal(barrier, inc=1, device_id=sibling, device_id_type=MESH)
    ta = o // 2
    for h in range(2):
        @pl.when(jnp.logical_or(ta != a, o != 2 * a + h))
        def _():
            pl.semaphore_signal(barrier, inc=1, device_id=dev(2 * a + h, ta), device_id_type=MESH)
    pl.semaphore_wait(barrier, occ_count + 1 + jnp.where(ta != a, 2, 1))

    def ky(r):
        return rcopy(f_ref.at[r], kbuf.at[c, y, r], ky_s.at[r], ky_r.at[r], y_peer)

    def ky_wait(r):
        rcopy(f_ref.at[r], kbuf.at[c, oy, r], ky_s.at[r], ky_r.at[r], y_peer).wait_recv()

    def ksib(n, yy, r):
        return rcopy(kbuf.at[c, yy, r], kbuf.at[c, yy, r], ksib_s.at[n], ksib_r.at[n], sibling)

    def ksib_wait(n, yy, r):
        rcopy(kbuf.at[oc, yy, r], kbuf.at[oc, yy, r], ksib_s.at[n], ksib_r.at[n], sibling).wait_recv()

    def item(oo, yy):
        return lbuf.at[oo, c, yy]

    def z_copy(d, zz, yy):
        oo = zz * 2 + x
        return rcopy(item(oo, yy), item(oo, yy), z_s.at[d, zz, yy], z_r.at[zz, yy], dev((z + 1 - 2 * d) * 2 + x, a))

    def x_copy(zz, yy):
        oo = zz * 2 + x
        return rcopy(item(oo, yy), item(oo, yy), x_s.at[zz, yy], x_r.at[zz, yy], x_peer)

    def x_wait(zz, yy):
        oo = zz * 2 + ox
        rcopy(item(oo, yy), item(oo, yy), x_s.at[zz, yy], x_r.at[zz, yy], x_peer).wait_recv()

    def s_copy(oo, yy):
        return rcopy(item(oo, yy), item(oo, yy), s_s.at[oo, yy], s_r.at[oo, yy], sibling)

    def s_wait(oo, yy):
        there = lbuf.at[oo, oc, yy]
        rcopy(there, there, s_s.at[oo, yy], s_r.at[oo, yy], sibling).wait_recv()

    zp = z + 1 - 2 * (z % 2)

    def by_z(zz, yy):
        return jnp.logical_and(zz == zp, yy == oy)

    def w_copy():
        there = item(z * 2 + ox, oy)
        return rcopy(there, there, w_s, w_r, dev(zp * 2 + x, a))

    def w_wait():
        there = item(zp * 2 + ox, oy)
        rcopy(there, there, w_s, w_r, dev(zp * 2 + x, a)).wait_recv()

    def forward(zz, yy, right, left):
        @pl.when(jnp.logical_and(right, z + 1 < lines))
        def _():
            z_copy(0, zz, yy).start()

        @pl.when(jnp.logical_and(left, z > 0))
        def _():
            z_copy(1, zz, yy).start()

        @pl.when(jnp.logical_not(by_z(zz, yy)))
        def _():
            x_copy(zz, yy).start()

        s_copy(zz * 2 + x, yy).start()

    def place(d, sign):
        zz = z - d + 2 * d * sign
        ok = jnp.logical_and(jnp.logical_and(zz >= 0, zz < lines), jnp.logical_or(d > 0, sign == 0))
        return zz, ok

    def stage(d, n):
        yy = (y + n) % 2
        for sign in range(2):
            zz, ok = place(d, sign)

            @pl.when(ok)
            def _():
                z_copy(0, zz, yy).wait_recv()
                forward(zz, yy, sign == 0, sign == 1)

    def across(d, n):
        yy = (y + n) % 2
        for sign in range(2):
            zz, ok = place(d, sign)

            @pl.when(jnp.logical_and(ok, jnp.logical_not(by_z(zz, yy))))
            def _():
                x_wait(zz, yy)
                s_copy(zz * 2 + ox, yy).start()

    loads[0].wait()
    ky(oy).start()
    lbuf[o, c, y] = f_ref[y]
    forward(z, y, True, True)
    ky(y).start()
    kbuf[c, y] = f_ref[...]
    ksib(0, y, 0).start()
    ksib(1, y, 1).start()
    for load in loads[1:]:
        load.wait()

    slots = i_ref.shape[1]
    order = lax.broadcasted_iota(jnp.int32, (8, slots), 1)
    row_hit = jnp.logical_and(
        i_ref[...] == lax.broadcasted_iota(jnp.int32, (8, slots), 0), order < count_ref[0]
    )
    col_hit = partner_ref[...] * held + j_ref[...] == lax.broadcasted_iota(jnp.int32, (128, slots), 0)
    cnt_ref[...] = nt(row_hit.astype(f32).astype(bf16), col_hit.astype(f32).astype(bf16))
    cnt[o] = cnt_ref[...]

    def cnt_copy(oo):
        return rcopy(cnt_ref, cnt.at[o], cnt_s.at[oo], cnt_r.at[o], dev(oo, a))

    for s in range(1, occ_count):
        cnt_copy((o + s) % occ_count).start()

    ky_wait(y)
    lbuf[o, c, oy] = kbuf[c, oy, y]
    forward(z, oy, True, True)
    ksib(2, oy, y).start()
    stage(1, 0)
    across(0, 0)
    ky_wait(oy)
    ksib(3, oy, oy).start()
    stage(1, 1)
    across(0, 1)

    gacc[...] = jnp.zeros_like(gacc)
    for s in range(1, occ_count):
        oo = (o + s) % occ_count
        rcopy(cnt_ref, cnt.at[oo], cnt_s.at[oo], cnt_r.at[oo], dev(oo, a)).wait_recv()
    ksib_wait(0, y, 0)
    ksib_wait(1, y, 1)
    ksib_wait(2, oy, y)
    ksib_wait(3, oy, oy)
    for cc in range(2):
        for yy in range(2):
            for k in range(2):
                kh[cc, yy, k * half:(k + 1) * half] = kbuf[cc, yy, k, pl.ds(c * half, half)]
    vcol = jnp.broadcast_to(v_ref[:, pl.ds(pl.multiple_of(c * half, half), half)], (width, half)).T
    side[0:half] = vcol - e_ref[0, 2 * o]
    side[half:virtuals] = vcol - e_ref[0, 2 * o + 1]
    vrow = v_ref[...]
    rows8 = lax.broadcasted_iota(jnp.int32, cnt_ref.shape, 0)
    lanes8 = lax.broadcasted_iota(jnp.int32, cnt_ref.shape, 1)

    def pick(tile, row, lane):
        here = jnp.logical_and(rows8 == row, lanes8 == lane)
        return jnp.sum(jnp.where(here, tile, 0.0), keepdims=True)

    def work(oo):
        far = 2 * oo + y
        inter = nt(kh[0, 0], lbuf[oo, 0, 0])
        inter += nt(kh[0, 1], lbuf[oo, 0, 1])
        inter += nt(kh[1, 0], lbuf[oo, 1, 0])
        inter += nt(kh[1, 1], lbuf[oo, 1, 1])
        amplitude = (inter / (side[...] + (vrow - e_ref[0, far]))).astype(bf16)
        mine, theirs = cnt[o], cnt[oo]
        w1 = [pick(mine, k, far) for k in range(2)]
        w2 = [pick(theirs, y, 2 * o + k) for k in range(2)]
        for cc in range(2):
            for yy in range(2):
                term = jnp.dot(amplitude, lbuf[oo, cc, yy], preferred_element_type=f32)
                for k in range(2):
                    part = term[k * half:(k + 1) * half]
                    gacc[cc, yy, k * half:(k + 1) * half] += (
                        w1[k] * part + w2[k] * part.astype(bf16).astype(f32)
                    )

    def column(d, ox_side):
        def each(sign, carry):
            zz, ok = place(d, sign)
            oo = zz * 2 + (x + ox_side) % 2

            @pl.when(jnp.logical_and(ok, jnp.logical_or(ox_side == 0, zz != zp)))
            def _():
                s_wait(oo, 0)
                s_wait(oo, 1)
                work(oo)

            return carry

        lax.fori_loop(0, 2, each, 0)

    column(0, 0)
    column(0, 1)

    def step(d, carry):
        def part(n, carry):
            @pl.when(d < lines)
            def _():
                stage(d, n)

            @pl.when(jnp.logical_and(d == 2, n == 1))
            def _():
                w_copy().start()

            across(d - 1, n)

            @pl.when(jnp.logical_and(d == lines, n == 1))
            def _():
                w_wait()
                s_copy(zp * 2 + ox, oy).start()

            column(d - 1, n)
            return carry

        return lax.fori_loop(0, 2, part, carry)

    lax.fori_loop(2, lines + 1, step, 0)
    s_wait(zp * 2 + ox, 0)
    s_wait(zp * 2 + ox, 1)
    work(zp * 2 + ox)

    out_width = aux_ref.shape[1]

    def cols(h):
        return slice(h * out_width, (h + 1) * out_width)

    def g_copy(h, cc):
        return rcopy(gsend.at[h, cc], grecv.at[h, cc], g_s.at[h, cc], g_r.at[h, cc], y_peer)

    def gs_copy(h):
        return rcopy(gfull.at[h], gsib.at[h], gs_s.at[h], gs_r.at[h], sibling)

    def ax_copy(h, b):
        return rcopy(axsend.at[h, b], axrecv.at[h, b], ax_s.at[h, b], ax_r.at[h, b], x_peer)

    def az_copy(h, b):
        return rcopy(azsend.at[h, b], azrecv.at[h, z], az_s.at[h, b], az_r.at[h, z], dev(b * 2 + x, a))

    def t_copy(h):
        return rcopy(tsend.at[h], trecv.at[o % 2], t_s.at[h], t_r.at[o % 2], dev(2 * a + h, ta))

    def t_far(h):
        return jnp.logical_or(ta != a, o != 2 * a + h)

    for h in range(2):
        for n in range(2):
            cc = (c + 1 + n) % 2
            gsend[h, cc] = gacc[cc, oy][:, cols(h)].astype(bf16)
            g_copy(h, cc).start()

    for h in range(2):
        g_copy(h, oc).wait_recv()
        gfull[h] = gacc[oc, y][:, cols(h)] + grecv[h, oc].astype(f32)
        gs_copy(h).start()
        g_copy(h, c).wait_recv()
        mine = gacc[c, y][:, cols(h)] + grecv[h, c].astype(f32)
        for k in range(2):
            gamma_ref[k, pl.ds(c * half, half), cols(h)] = mine[k * half:(k + 1) * half]
        gs_copy(h).wait_recv()
        for k in range(2):
            gamma_ref[k, pl.ds(oc * half, half), cols(h)] = gsib[h, k * half:(k + 1) * half]
        rounded = gamma_ref[:, :, cols(h)].reshape(held * virtuals, out_width).astype(bf16)

        for block in ((z + 2) % 4, (z + 3 + 2 * (z % 2)) % 4, zp, z):
            terms = tn(rounded, kbuf[block % 2, block // 2].reshape(held * virtuals, width))
            low, high = terms[:, cols(0)], terms[:, cols(1)]
            axsend[h, block] = jnp.where(x == 0, high, low).astype(bf16)
            ax_copy(h, block).start()
            akeep[h, block] = jnp.where(x == 0, low, high)

    across_z = (z + 3 + 2 * (z % 2)) % 4

    def near_copy(h):
        return rcopy(near.at[h], nearin.at[h], n_s.at[h], n_r.at[h], dev(zp * 2 + x, a))

    def pair_sum(h, block):
        ax_copy(h, block).wait_recv()
        return akeep[h, block] + axrecv[h, block].astype(f32)

    for h in range(2):
        for block in ((z + 2) % 4, across_z):
            azsend[h, block] = pair_sum(h, block).astype(bf16)
            az_copy(h, block).start()
        near[h] = pair_sum(h, zp)
        near_copy(h).start()
        akeep[h, z] = pair_sum(h, z)

    for h in range(2):
        total = akeep[h, z]
        for zz in ((z + 2) % 4, across_z):
            rcopy(azsend.at[h, zz], azrecv.at[h, zz], az_s.at[h, zz], az_r.at[h, zz], dev(zz * 2 + x, a)).wait_recv()
            total += azrecv[h, zz].astype(f32)
        near_copy(h).wait_recv()
        total += nearin[h]
        tsend[h] = total

        @pl.when(t_far(h))
        def _():
            t_copy(h).start()

        @pl.when(jnp.logical_not(t_far(h)))
        def _():
            trecv[o % 2] = tsend[h]

    scale = float(occ_count * held * virtuals) ** (-0.5)
    for h in range(2):
        @pl.when(t_far(h))
        def _():
            rcopy(tsend.at[h], trecv.at[h], t_s.at[h], t_r.at[h], dev(2 * a + h, ta)).wait_recv()

        aux_ref[cols(h)] = (tsend[h] + trecv[h].T) * scale

    w_copy().wait_send()
    for r in range(2):
        ky(r).wait_send()
        g_copy(r, 0).wait_send()
        g_copy(r, 1).wait_send()
        gs_copy(r).wait_send()
    ksib(0, y, 0).wait_send()
    ksib(1, y, 1).wait_send()
    ksib(2, oy, y).wait_send()
    ksib(3, oy, oy).wait_send()
    for s in range(1, occ_count):
        oo = (o + s) % occ_count
        cnt_copy(oo).wait_send()
    for h in range(2):
        @pl.when(t_far(h))
        def _():
            t_copy(h).wait_send()

        for n in range(lines):
            block = (z + n) % lines
            ax_copy(h, block).wait_send()

        az_copy(h, (z + 2) % 4).wait_send()
        az_copy(h, across_z).wait_send()
        near_copy(h).wait_send()

    def drain(zz, carry):
        for yy in range(2):
            @pl.when(jnp.logical_and(zz <= z, z + 1 < lines))
            def _():
                z_copy(0, zz, yy).wait_send()

            @pl.when(jnp.logical_and(zz >= z, z > 0))
            def _():
                z_copy(1, zz, yy).wait_send()

            @pl.when(jnp.logical_not(by_z(zz, yy)))
            def _():
                x_copy(zz, yy).wait_send()

            s_copy(zz * 2, yy).wait_send()
            s_copy(zz * 2 + 1, yy).wait_send()
        return carry

    lax.fori_loop(0, lines, drain, 0)


def table_body(factors, occ_energy, vir_energy, i_slot, j_slot, partner_device, pair_count):
    held, virtuals, width = factors.shape
    slots = i_slot.shape[0]
    orbitals = occ_energy.shape[0]
    occ_count = lax.axis_size("occ")
    lines = occ_count // 2
    out_width = 4 * width // occ_count
    vmem = pl.BlockSpec(memory_space=pltpu.VMEM)
    dma = pltpu.SemaphoreType.DMA
    return pl.pallas_call(
        kernel,
        out_shape=(
            jax.ShapeDtypeStruct((held, virtuals, width), f32),
            jax.ShapeDtypeStruct((width, out_width), f32),
        ),
        in_specs=[pl.BlockSpec(memory_space=pltpu.HBM)] * 6 + [pl.BlockSpec(memory_space=pltpu.SMEM)],
        out_specs=(vmem, vmem),
        scratch_shapes=[
            pltpu.VMEM((2, 2, held, virtuals, width), bf16),
            pltpu.VMEM((occ_count, 2, 2, virtuals, width), bf16),
            pltpu.VMEM((2, 2, virtuals, width), bf16),
            pltpu.VMEM((occ_count, 8, 128), f32),
            pltpu.VMEM((2, 2, virtuals, width), f32),
            pltpu.VMEM((2, 2, virtuals, out_width), bf16),
            pltpu.VMEM((2, 2, virtuals, out_width), bf16),
            pltpu.VMEM((2, virtuals, out_width), f32),
            pltpu.VMEM((2, virtuals, out_width), f32),
            pltpu.VMEM((2, lines, out_width, out_width), bf16),
            pltpu.VMEM((2, lines, out_width, out_width), bf16),
            pltpu.VMEM((2, lines, out_width, out_width), f32),
            pltpu.VMEM((2, lines, out_width, out_width), bf16),
            pltpu.VMEM((2, lines, out_width, out_width), bf16),
            pltpu.VMEM((2, out_width, out_width), f32),
            pltpu.VMEM((2, out_width, out_width), f32),
            pltpu.VMEM((2, out_width, out_width), f32),
            pltpu.VMEM((2, out_width, out_width), f32),
            dma((2,)), dma((2,)), dma((4,)), dma((4,)),
            dma((2, lines, 2)), dma((lines, 2)), dma((lines, 2)), dma((lines, 2)),
            dma((occ_count, 2)), dma((occ_count, 2)),
            dma((occ_count,)), dma((occ_count,)), dma((2, 2)), dma((2, 2)), dma((2,)), dma((2,)),
            dma((2, lines)), dma((2, lines)), dma((2, lines)), dma((2, lines)), dma((2,)), dma((2,)), dma, dma, dma((2,)), dma((2,)),
            pltpu.VMEM((held, virtuals, width), bf16),
            pltpu.SMEM((1, orbitals), f32),
            pltpu.VMEM((1, virtuals), f32),
            pltpu.VMEM((1, slots), jnp.int32),
            pltpu.VMEM((1, slots), jnp.int32),
            pltpu.VMEM((1, slots), jnp.int32),
            pltpu.VMEM((8, 128), f32),
            pltpu.VMEM((virtuals, virtuals), f32),
            dma((6,)),
        ],
        compiler_params=pltpu.CompilerParams(
            collective_id=0, has_side_effects=True, vmem_limit_bytes=64 * 1024 * 1024
        ),
    )(
        factors, occ_energy[None, :], vir_energy[None, :], i_slot[None, :], j_slot[None, :],
        partner_device.reshape(1, slots), pair_count,
    )


def body(*operands):
    factors, i_slot = operands[0], operands[3]
    held, virtuals, width = factors.shape
    occ_count, aux_count = lax.axis_size("occ"), lax.axis_size("aux")
    orbitals = held * occ_count
    fits = (
        held == 2 and aux_count == 4 and occ_count == 2 * aux_count and orbitals <= 128
        and orbitals * orbitals <= occ_count * i_slot.shape[0]
        and virtuals == width and width % 256 == 0 and 4 * width == occ_count * 128
    )
    return table_body(*operands) if fits else slot_body(*operands)


def solution(mesh):
    placed = (P("occ", None, "aux"), P(), P(), P("occ"), P("occ"), P("occ", None), P("occ"))
    return jax.shard_map(
        body,
        mesh=mesh,
        in_specs=placed,
        out_specs=(P("occ", None, "aux"), P("aux", "occ")),
        check_vma=False,
    )
```

```python
import jax
import jax.numpy as jnp
from jax import lax
from jax.experimental import pallas as pl
from jax.experimental.pallas import tpu as pltpu
from jax.sharding import PartitionSpec as P

MESH = pl.DeviceIdType.MESH
f32 = jnp.float32
bf16 = jnp.bfloat16


def slot_body(factors, occ_energy, vir_energy, i_slot, j_slot, partner_device, pair_count):
    held, virtuals, columns = factors.shape
    pair_slots = i_slot.shape[0]
    occ_count = lax.axis_size("occ")
    capacity = max(2, (3 * pair_slots // 2 + occ_count - 1) // occ_count)
    slot_total = occ_count * capacity
    device_index = lax.axis_index("occ")
    pair_order = jnp.arange(pair_slots, dtype=jnp.int32)
    living = pair_order < pair_count[0]
    target = partner_device[:, 0]
    earlier = (
        (target[:, None] == target[None, :])
        & living[None, :]
        & (pair_order[None, :] < pair_order[:, None])
    )
    slot_rank = jnp.sum(earlier.astype(jnp.int32), axis=1)
    slot_index = target * capacity + slot_rank
    slot_hit = (slot_index[:, None] == jnp.arange(slot_total, dtype=jnp.int32)[None, :]) & living[
        :, None
    ]
    requests = jnp.sum(jnp.where(slot_hit, j_slot[:, None] + 1, 0), axis=0) - 1
    wanted = lax.all_to_all(requests, "occ", split_axis=0, concat_axis=0, tiled=True)
    wanted_hit = (wanted[:, None] == jnp.arange(held, dtype=jnp.int32)[None, :]).astype(
        jnp.bfloat16
    )
    far_index = target * held + j_slot
    piece = lax.all_gather(factors, "occ", axis=0, tiled=True)
    count = piece.shape[0]
    hit = (far_index[:, None] == jnp.arange(count, dtype=jnp.int32)[None, :]).astype(jnp.bfloat16)
    gathered = jnp.dot(
        hit, piece.reshape(count, virtuals * columns), preferred_element_type=jnp.float32
    )
    partner_blocks = gathered.astype(jnp.bfloat16).reshape(pair_slots, virtuals, columns)
    own_blocks = factors[i_slot]
    orbitals = occ_energy.shape[0]
    table = jnp.arange(orbitals, dtype=jnp.int32)
    own_index = device_index * held + i_slot
    energy_own = jnp.sum(
        jnp.where(own_index[:, None] == table[None, :], occ_energy[None, :], 0.0), axis=1
    )
    energy_far = jnp.sum(
        jnp.where(far_index[:, None] == table[None, :], occ_energy[None, :], 0.0), axis=1
    )
    denominator = (
        vir_energy[None, :, None]
        + vir_energy[None, None, :]
        - energy_own[:, None, None]
        - energy_far[:, None, None]
    )
    partial_value = jnp.einsum(
        "pvq,pwq->pvw", own_blocks, partner_blocks, preferred_element_type=jnp.float32
    )
    summed = lax.psum(partial_value, "aux")
    amplitude = jnp.where(living[:, None, None], summed / denominator, 0.0).astype(jnp.bfloat16)
    local_terms = jnp.einsum(
        "pvw,pwq->pvq", amplitude, partner_blocks, preferred_element_type=jnp.float32
    )
    owner_hit = (i_slot[:, None] == jnp.arange(held, dtype=jnp.int32)[None, :]).astype(jnp.float32)
    gamma_local = jnp.einsum("po,pvq->ovq", owner_hit, local_terms, precision=lax.Precision.HIGHEST)
    return_terms = jnp.einsum(
        "pwv,pwq->pvq", amplitude, own_blocks, preferred_element_type=jnp.float32
    ).astype(jnp.bfloat16)
    placed = jnp.dot(
        slot_hit.astype(jnp.bfloat16).T,
        return_terms.reshape(pair_slots, virtuals * columns),
        preferred_element_type=jnp.float32,
    )
    placed = placed.astype(jnp.bfloat16).reshape(slot_total, virtuals, columns)
    returned = lax.all_to_all(placed, "occ", split_axis=0, concat_axis=0, tiled=True)
    gathered_back = jnp.dot(
        wanted_hit.T,
        returned.reshape(slot_total, virtuals * columns),
        preferred_element_type=jnp.float32,
    )
    gamma = gamma_local + gathered_back.reshape(held, virtuals, columns)
    rounded = gamma.astype(jnp.bfloat16)
    stacked = jnp.stack([rounded, factors])
    gamma_rows = rounded.reshape(held * virtuals, columns)
    factor_flat = factors.reshape(held * virtuals, columns)
    piece = lax.all_gather(stacked, "aux", axis=3, tiled=True)
    width_here = piece.shape[3]
    gamma_piece = piece[0].reshape(held * virtuals, width_here)
    factor_piece = piece[1].reshape(held * virtuals, width_here)
    first = jnp.dot(gamma_rows.T, factor_piece, preferred_element_type=jnp.float32)
    second = jnp.dot(factor_flat.T, gamma_piece, preferred_element_type=jnp.float32)
    terms = first + second
    shared = lax.psum_scatter(terms, "occ", scatter_dimension=1, tiled=True)
    factor_scale = float(orbitals * virtuals) ** (-0.5)
    return (gamma, shared * factor_scale)


def nt(a, b):
    return lax.dot_general(a, b, (((1,), (1,)), ((), ())), preferred_element_type=f32)


def tn(a, b):
    return lax.dot_general(a, b, (((0,), (0,)), ((), ())), preferred_element_type=f32)


def kernel(
    f_hbm, e_hbm, v_hbm, i_hbm, j_hbm, partner_hbm, count_ref,
    gamma_ref, aux_ref,
    kbuf, lbuf, kh, cnt, gacc, gsend, grecv, gfull, gsib, axsend, axrecv, akeep, azsend, azrecv, near, nearin, tsend, trecv,
    ky_s, ky_r, ksib_s, ksib_r, z_s, z_r, x_s, x_r, s_s, s_r,
    cnt_s, cnt_r, g_s, g_r, gs_s, gs_r, ax_s, ax_r, az_s, az_r, t_s, t_r, n_s, n_r,
    f_ref, e_ref, v_ref, i_ref, j_ref, partner_ref, cnt_ref, side, in_s,
):
    occ_count = lax.axis_size("occ")
    lines = occ_count // 2
    held, virtuals, width = f_ref.shape
    half = virtuals // 2
    o = lax.axis_index("occ")
    a = lax.axis_index("aux")
    z, x = o // 2, o % 2
    y, c = a // 2, a % 2
    oy, oc, ox = 1 - y, 1 - c, 1 - x

    def dev(occ, aux):
        return {"occ": occ, "aux": aux}

    y_peer, sibling = dev(o, oy * 2 + c), dev(o, y * 2 + oc)
    x_peer = dev(z * 2 + ox, a)

    def rcopy(src, dst, ss, rs, target):
        return pltpu.make_async_remote_copy(
            src_ref=src, dst_ref=dst, send_sem=ss, recv_sem=rs, device_id=target, device_id_type=MESH
        )

    pairs = (
        (f_hbm, f_ref), (e_hbm, e_ref), (v_hbm, v_ref), (i_hbm, i_ref), (j_hbm, j_ref),
        (partner_hbm, partner_ref),
    )
    loads = [pltpu.make_async_copy(there, here, in_s.at[n]) for n, (there, here) in enumerate(pairs)]
    for load in loads:
        load.start()

    barrier = pltpu.get_barrier_semaphore()
    for s in range(1, occ_count):
        pl.semaphore_signal(barrier, inc=1, device_id=dev((o + s) % occ_count, a), device_id_type=MESH)
    pl.semaphore_signal(barrier, inc=1, device_id=y_peer, device_id_type=MESH)
    pl.semaphore_signal(barrier, inc=1, device_id=sibling, device_id_type=MESH)
    ta = o // 2
    for h in range(2):
        @pl.when(jnp.logical_or(ta != a, o != 2 * a + h))
        def _():
            pl.semaphore_signal(barrier, inc=1, device_id=dev(2 * a + h, ta), device_id_type=MESH)
    pl.semaphore_wait(barrier, occ_count + 1 + jnp.where(ta != a, 2, 1))

    def ky(r):
        return rcopy(f_ref.at[r], kbuf.at[c, y, r], ky_s.at[r], ky_r.at[r], y_peer)

    def ky_wait(r):
        rcopy(f_ref.at[r], kbuf.at[c, oy, r], ky_s.at[r], ky_r.at[r], y_peer).wait_recv()

    def ksib(n, yy, r):
        return rcopy(kbuf.at[c, yy, r], kbuf.at[c, yy, r], ksib_s.at[n], ksib_r.at[n], sibling)

    def ksib_wait(n, yy, r):
        rcopy(kbuf.at[oc, yy, r], kbuf.at[oc, yy, r], ksib_s.at[n], ksib_r.at[n], sibling).wait_recv()

    def item(oo, yy):
        return lbuf.at[oo, c, yy]

    def z_copy(d, zz, yy):
        oo = zz * 2 + x
        return rcopy(item(oo, yy), item(oo, yy), z_s.at[d, zz, yy], z_r.at[zz, yy], dev((z + 1 - 2 * d) * 2 + x, a))

    def x_copy(zz, yy):
        oo = zz * 2 + x
        return rcopy(item(oo, yy), item(oo, yy), x_s.at[zz, yy], x_r.at[zz, yy], x_peer)

    def x_wait(zz, yy):
        oo = zz * 2 + ox
        rcopy(item(oo, yy), item(oo, yy), x_s.at[zz, yy], x_r.at[zz, yy], x_peer).wait_recv()

    def s_copy(oo, yy):
        return rcopy(item(oo, yy), item(oo, yy), s_s.at[oo, yy], s_r.at[oo, yy], sibling)

    def s_wait(oo, yy):
        there = lbuf.at[oo, oc, yy]
        rcopy(there, there, s_s.at[oo, yy], s_r.at[oo, yy], sibling).wait_recv()

    zp = z + 1 - 2 * (z % 2)

    def forward(zz, yy, right, left):
        @pl.when(jnp.logical_and(right, z + 1 < lines))
        def _():
            z_copy(0, zz, yy).start()

        @pl.when(jnp.logical_and(left, z > 0))
        def _():
            z_copy(1, zz, yy).start()

        x_copy(zz, yy).start()
        s_copy(zz * 2 + x, yy).start()

    def place(d, sign):
        zz = z - d + 2 * d * sign
        ok = jnp.logical_and(jnp.logical_and(zz >= 0, zz < lines), jnp.logical_or(d > 0, sign == 0))
        return zz, ok

    def stage(d, n):
        yy = (y + n) % 2
        for sign in range(2):
            zz, ok = place(d, sign)

            @pl.when(ok)
            def _():
                z_copy(0, zz, yy).wait_recv()
                forward(zz, yy, sign == 0, sign == 1)

    def across(d, n):
        yy = (y + n) % 2
        for sign in range(2):
            zz, ok = place(d, sign)

            @pl.when(ok)
            def _():
                x_wait(zz, yy)
                s_copy(zz * 2 + ox, yy).start()

    loads[0].wait()
    ky(oy).start()
    lbuf[o, c, y] = f_ref[y]
    forward(z, y, True, True)
    ky(y).start()
    kbuf[c, y] = f_ref[...]
    ksib(0, y, 0).start()
    ksib(1, y, 1).start()
    for load in loads[1:]:
        load.wait()

    slots = i_ref.shape[1]
    order = lax.broadcasted_iota(jnp.int32, (8, slots), 1)
    row_hit = jnp.logical_and(
        i_ref[...] == lax.broadcasted_iota(jnp.int32, (8, slots), 0), order < count_ref[0]
    )
    col_hit = partner_ref[...] * held + j_ref[...] == lax.broadcasted_iota(jnp.int32, (128, slots), 0)
    cnt_ref[...] = nt(row_hit.astype(f32).astype(bf16), col_hit.astype(f32).astype(bf16))
    cnt[o] = cnt_ref[...]

    def cnt_copy(oo):
        return rcopy(cnt_ref, cnt.at[o], cnt_s.at[oo], cnt_r.at[o], dev(oo, a))

    for s in range(1, occ_count):
        cnt_copy((o + s) % occ_count).start()

    ky_wait(y)
    lbuf[o, c, oy] = kbuf[c, oy, y]
    forward(z, oy, True, True)
    ksib(2, oy, y).start()
    stage(1, 0)
    across(0, 0)
    ky_wait(oy)
    ksib(3, oy, oy).start()
    stage(1, 1)
    across(0, 1)

    gacc[...] = jnp.zeros_like(gacc)
    for s in range(1, occ_count):
        oo = (o + s) % occ_count
        rcopy(cnt_ref, cnt.at[oo], cnt_s.at[oo], cnt_r.at[oo], dev(oo, a)).wait_recv()
    ksib_wait(0, y, 0)
    ksib_wait(1, y, 1)
    ksib_wait(2, oy, y)
    ksib_wait(3, oy, oy)
    for cc in range(2):
        for yy in range(2):
            for k in range(2):
                kh[cc, yy, k * half:(k + 1) * half] = kbuf[cc, yy, k, pl.ds(c * half, half)]
    vcol = jnp.broadcast_to(v_ref[:, pl.ds(pl.multiple_of(c * half, half), half)], (width, half)).T
    side[0:half] = vcol - e_ref[0, 2 * o]
    side[half:virtuals] = vcol - e_ref[0, 2 * o + 1]
    vrow = v_ref[...]
    rows8 = lax.broadcasted_iota(jnp.int32, cnt_ref.shape, 0)
    lanes8 = lax.broadcasted_iota(jnp.int32, cnt_ref.shape, 1)

    def pick(tile, row, lane):
        here = jnp.logical_and(rows8 == row, lanes8 == lane)
        return jnp.sum(jnp.where(here, tile, 0.0), keepdims=True)

    def work(oo):
        far = 2 * oo + y
        inter = nt(kh[0, 0], lbuf[oo, 0, 0])
        inter += nt(kh[0, 1], lbuf[oo, 0, 1])
        inter += nt(kh[1, 0], lbuf[oo, 1, 0])
        inter += nt(kh[1, 1], lbuf[oo, 1, 1])
        amplitude = (inter / (side[...] + (vrow - e_ref[0, far]))).astype(bf16)
        mine, theirs = cnt[o], cnt[oo]
        w1 = [pick(mine, k, far) for k in range(2)]
        w2 = [pick(theirs, y, 2 * o + k) for k in range(2)]
        for cc in range(2):
            for yy in range(2):
                term = jnp.dot(amplitude, lbuf[oo, cc, yy], preferred_element_type=f32)
                for k in range(2):
                    part = term[k * half:(k + 1) * half]
                    gacc[cc, yy, k * half:(k + 1) * half] += (
                        w1[k] * part + w2[k] * part.astype(bf16).astype(f32)
                    )

    def column(d, ox_side):
        def each(sign, carry):
            zz, ok = place(d, sign)
            oo = zz * 2 + (x + ox_side) % 2

            @pl.when(ok)
            def _():
                s_wait(oo, 0)
                s_wait(oo, 1)
                work(oo)

            return carry

        lax.fori_loop(0, 2, each, 0)

    column(0, 0)
    column(0, 1)

    def step(d, carry):
        def part(n, carry):
            @pl.when(d < lines)
            def _():
                stage(d, n)

            across(d - 1, n)
            column(d - 1, n)
            return carry

        return lax.fori_loop(0, 2, part, carry)

    lax.fori_loop(2, lines + 1, step, 0)

    out_width = aux_ref.shape[1]

    def cols(h):
        return slice(h * out_width, (h + 1) * out_width)

    def g_copy(h, cc):
        return rcopy(gsend.at[h, cc], grecv.at[h, cc], g_s.at[h, cc], g_r.at[h, cc], y_peer)

    def gs_copy(h):
        return rcopy(gfull.at[h], gsib.at[h], gs_s.at[h], gs_r.at[h], sibling)

    def ax_copy(h, b):
        return rcopy(axsend.at[h, b], axrecv.at[h, b], ax_s.at[h, b], ax_r.at[h, b], x_peer)

    def az_copy(h, b):
        return rcopy(azsend.at[h, b], azrecv.at[h, z], az_s.at[h, b], az_r.at[h, z], dev(b * 2 + x, a))

    def t_copy(h):
        return rcopy(tsend.at[h], trecv.at[o % 2], t_s.at[h], t_r.at[o % 2], dev(2 * a + h, ta))

    def t_far(h):
        return jnp.logical_or(ta != a, o != 2 * a + h)

    for h in range(2):
        for n in range(2):
            cc = (c + 1 + n) % 2
            gsend[h, cc] = gacc[cc, oy][:, cols(h)].astype(bf16)
            g_copy(h, cc).start()

    for h in range(2):
        g_copy(h, oc).wait_recv()
        gfull[h] = gacc[oc, y][:, cols(h)] + grecv[h, oc].astype(f32)
        gs_copy(h).start()
        g_copy(h, c).wait_recv()
        mine = gacc[c, y][:, cols(h)] + grecv[h, c].astype(f32)
        for k in range(2):
            gamma_ref[k, pl.ds(c * half, half), cols(h)] = mine[k * half:(k + 1) * half]
        gs_copy(h).wait_recv()
        for k in range(2):
            gamma_ref[k, pl.ds(oc * half, half), cols(h)] = gsib[h, k * half:(k + 1) * half]
        rounded = gamma_ref[:, :, cols(h)].reshape(held * virtuals, out_width).astype(bf16)

        for block in ((z + 2) % 4, (z + 3 + 2 * (z % 2)) % 4, zp, z):
            terms = tn(rounded, kbuf[block % 2, block // 2].reshape(held * virtuals, width))
            low, high = terms[:, cols(0)], terms[:, cols(1)]
            axsend[h, block] = jnp.where(x == 0, high, low).astype(bf16)
            ax_copy(h, block).start()
            akeep[h, block] = jnp.where(x == 0, low, high)

    across_z = (z + 3 + 2 * (z % 2)) % 4

    def near_copy(h):
        return rcopy(near.at[h], nearin.at[h], n_s.at[h], n_r.at[h], dev(zp * 2 + x, a))

    def pair_sum(h, block):
        ax_copy(h, block).wait_recv()
        return akeep[h, block] + axrecv[h, block].astype(f32)

    for h in range(2):
        for block in ((z + 2) % 4, across_z):
            azsend[h, block] = pair_sum(h, block).astype(bf16)
            az_copy(h, block).start()
        near[h] = pair_sum(h, zp)
        near_copy(h).start()
        akeep[h, z] = pair_sum(h, z)

    for h in range(2):
        total = akeep[h, z]
        for zz in ((z + 2) % 4, across_z):
            rcopy(azsend.at[h, zz], azrecv.at[h, zz], az_s.at[h, zz], az_r.at[h, zz], dev(zz * 2 + x, a)).wait_recv()
            total += azrecv[h, zz].astype(f32)
        near_copy(h).wait_recv()
        total += nearin[h]
        tsend[h] = total

        @pl.when(t_far(h))
        def _():
            t_copy(h).start()

        @pl.when(jnp.logical_not(t_far(h)))
        def _():
            trecv[o % 2] = tsend[h]

    scale = float(occ_count * held * virtuals) ** (-0.5)
    for h in range(2):
        @pl.when(t_far(h))
        def _():
            rcopy(tsend.at[h], trecv.at[h], t_s.at[h], t_r.at[h], dev(2 * a + h, ta)).wait_recv()

        aux_ref[cols(h)] = (tsend[h] + trecv[h].T) * scale

    for r in range(2):
        ky(r).wait_send()
        g_copy(r, 0).wait_send()
        g_copy(r, 1).wait_send()
        gs_copy(r).wait_send()
    ksib(0, y, 0).wait_send()
    ksib(1, y, 1).wait_send()
    ksib(2, oy, y).wait_send()
    ksib(3, oy, oy).wait_send()
    for s in range(1, occ_count):
        oo = (o + s) % occ_count
        cnt_copy(oo).wait_send()
    for h in range(2):
        @pl.when(t_far(h))
        def _():
            t_copy(h).wait_send()

        for n in range(lines):
            block = (z + n) % lines
            ax_copy(h, block).wait_send()

        az_copy(h, (z + 2) % 4).wait_send()
        az_copy(h, across_z).wait_send()
        near_copy(h).wait_send()

    def drain(zz, carry):
        for yy in range(2):
            @pl.when(jnp.logical_and(zz <= z, z + 1 < lines))
            def _():
                z_copy(0, zz, yy).wait_send()

            @pl.when(jnp.logical_and(zz >= z, z > 0))
            def _():
                z_copy(1, zz, yy).wait_send()

            x_copy(zz, yy).wait_send()
            s_copy(zz * 2, yy).wait_send()
            s_copy(zz * 2 + 1, yy).wait_send()
        return carry

    lax.fori_loop(0, lines, drain, 0)


def table_body(factors, occ_energy, vir_energy, i_slot, j_slot, partner_device, pair_count):
    held, virtuals, width = factors.shape
    slots = i_slot.shape[0]
    orbitals = occ_energy.shape[0]
    occ_count = lax.axis_size("occ")
    lines = occ_count // 2
    out_width = 4 * width // occ_count
    vmem = pl.BlockSpec(memory_space=pltpu.VMEM)
    dma = pltpu.SemaphoreType.DMA
    return pl.pallas_call(
        kernel,
        out_shape=(
            jax.ShapeDtypeStruct((held, virtuals, width), f32),
            jax.ShapeDtypeStruct((width, out_width), f32),
        ),
        in_specs=[pl.BlockSpec(memory_space=pltpu.HBM)] * 6 + [pl.BlockSpec(memory_space=pltpu.SMEM)],
        out_specs=(vmem, vmem),
        scratch_shapes=[
            pltpu.VMEM((2, 2, held, virtuals, width), bf16),
            pltpu.VMEM((occ_count, 2, 2, virtuals, width), bf16),
            pltpu.VMEM((2, 2, virtuals, width), bf16),
            pltpu.VMEM((occ_count, 8, 128), f32),
            pltpu.VMEM((2, 2, virtuals, width), f32),
            pltpu.VMEM((2, 2, virtuals, out_width), bf16),
            pltpu.VMEM((2, 2, virtuals, out_width), bf16),
            pltpu.VMEM((2, virtuals, out_width), f32),
            pltpu.VMEM((2, virtuals, out_width), f32),
            pltpu.VMEM((2, lines, out_width, out_width), bf16),
            pltpu.VMEM((2, lines, out_width, out_width), bf16),
            pltpu.VMEM((2, lines, out_width, out_width), f32),
            pltpu.VMEM((2, lines, out_width, out_width), bf16),
            pltpu.VMEM((2, lines, out_width, out_width), bf16),
            pltpu.VMEM((2, out_width, out_width), f32),
            pltpu.VMEM((2, out_width, out_width), f32),
            pltpu.VMEM((2, out_width, out_width), f32),
            pltpu.VMEM((2, out_width, out_width), f32),
            dma((2,)), dma((2,)), dma((4,)), dma((4,)),
            dma((2, lines, 2)), dma((lines, 2)), dma((lines, 2)), dma((lines, 2)),
            dma((occ_count, 2)), dma((occ_count, 2)),
            dma((occ_count,)), dma((occ_count,)), dma((2, 2)), dma((2, 2)), dma((2,)), dma((2,)),
            dma((2, lines)), dma((2, lines)), dma((2, lines)), dma((2, lines)), dma((2,)), dma((2,)), dma((2,)), dma((2,)),
            pltpu.VMEM((held, virtuals, width), bf16),
            pltpu.SMEM((1, orbitals), f32),
            pltpu.VMEM((1, virtuals), f32),
            pltpu.VMEM((1, slots), jnp.int32),
            pltpu.VMEM((1, slots), jnp.int32),
            pltpu.VMEM((1, slots), jnp.int32),
            pltpu.VMEM((8, 128), f32),
            pltpu.VMEM((virtuals, virtuals), f32),
            dma((6,)),
        ],
        compiler_params=pltpu.CompilerParams(
            collective_id=0, has_side_effects=True, vmem_limit_bytes=64 * 1024 * 1024
        ),
    )(
        factors, occ_energy[None, :], vir_energy[None, :], i_slot[None, :], j_slot[None, :],
        partner_device.reshape(1, slots), pair_count,
    )


def body(*operands):
    factors, i_slot = operands[0], operands[3]
    held, virtuals, width = factors.shape
    occ_count, aux_count = lax.axis_size("occ"), lax.axis_size("aux")
    orbitals = held * occ_count
    fits = (
        held == 2 and aux_count == 4 and occ_count == 2 * aux_count and orbitals <= 128
        and orbitals * orbitals <= occ_count * i_slot.shape[0]
        and virtuals == width and width % 256 == 0 and 4 * width == occ_count * 128
    )
    return table_body(*operands) if fits else slot_body(*operands)


def solution(mesh):
    placed = (P("occ", None, "aux"), P(), P(), P("occ"), P("occ"), P("occ", None), P("occ"))
    return jax.shard_map(
        body,
        mesh=mesh,
        in_specs=placed,
        out_specs=(P("occ", None, "aux"), P("aux", "occ")),
        check_vma=False,
    )
```
